128 devices in a mesh: row: 16 (over y, z), col: 8 (over x, core).
Axes of the slice: x: 4, y: 4, z: 4, core: 2. Of those that a mesh axis runs over, the one named last changes fastest.
Arguments:
- front: float32 [6, 16, 128, 12, 8, 128], P(None, 'row', None, None, 'col'), may hold values from -2.01 to 16, as said below
- child_updates: float32 [6, 16, 128, 6, 8, 128], P(None, 'row', None, None, 'col'), may hold values from -0.5 to 0.005, as said below
- child_maps: int32 [2, 48], replicated, may hold values from 0 to 62, as said below
- child_orders: int32 [2], replicated, may hold values from 6017 to 6144, as said below
Outputs:
- factored: float32 [6, 16, 128, 12, 8, 128], P(None, 'row', None, None, 'col')
The draws below stay inside these ranges and needn't reach their ends.
Inputs may be any that keep to these rules, and one draw needn't show every extreme that they name: `front`: symmetric; with the children's updates added as above it is positive definite. `child_updates`: each child's update is symmetric. `child_maps`: each child's map adds to a tile's index an offset that is the same over aligned runs of 8 child tiles, rises strictly from run to run, is 0 on the first run and 15 on the last, and differs modulo 8 between runs. `child_orders`: each order lies in the last tile of its padded update; one of the two is 6144.
All inputs are finite; a program needn't handle non-finite values.
Results may differ from the reference program's by a relative error of at most 0.00005.
Values sent between devices are 32-bit elements; how exact they have to be, the bound alone decides.
No kernel may reach another device: no remote copies, remote signals or barrier semaphores. Data moves between devices by JAX's collectives and lax.ppermute only.
A program may use at most 128 MiB of HBM per device.

```python
import math
import jax
import jax.numpy as jnp
from jax import lax

TILE = 128
FT = 96
CT = 48
PT = 5
PANELS = 1
RUN = 8
N_ROW = 16
N_COL = 8


def shift_down(values, count):
    return jnp.concatenate([jnp.zeros((count,), jnp.float32), values[:-count]])


def draw_front(key, part):
    front_order = FT * TILE
    layers = front_order // 256
    perm_key, weight_key, shift_key, fill_key = jax.random.split(key, 4)
    cells = jax.random.permutation(perm_key, front_order).astype(jnp.int32)
    weights = jnp.exp(jax.random.uniform(weight_key, (3, front_order), jnp.float32, math.log(0.4), math.log(2.0)))
    shifts = jax.random.uniform(shift_key, (front_order,), jnp.float32, 2.0, 3.0)
    fill = jax.random.uniform(fill_key, (front_order, front_order), jnp.float32, -0.001, 0.001)
    grid_cells = jnp.arange(front_order, dtype=jnp.int32)
    along_x = jnp.where(grid_cells // 256 < layers - 1, weights[0], 0.0).astype(jnp.float32)
    along_y = jnp.where(grid_cells // 16 % 16 < 15, weights[1], 0.0).astype(jnp.float32)
    along_z = jnp.where(grid_cells % 16 < 15, weights[2], 0.0).astype(jnp.float32)
    degree = along_x + along_y + along_z + shift_down(along_x, 256) + shift_down(along_y, 16) + shift_down(along_z, 1)
    index_x = along_x[cells]
    index_y = along_y[cells]
    index_z = along_z[cells]
    row_cells = cells[:, None]
    col_cells = cells[None, :]
    first = row_cells < col_cells
    gap = jnp.abs(row_cells - col_cells)

    def pick(values):
        return jnp.where(first, values[:, None], values[None, :])
    edge = jnp.where(gap == 256, pick(index_x), jnp.where(gap == 16, pick(index_y), jnp.where(gap == 1, pick(index_z), 0.0)))
    symmetric_fill = 0.5 * (fill + fill.T)
    pivots = degree[cells] + shifts
    full_matrix = jnp.where(gap == 0, pivots[:, None], symmetric_fill - edge)
    return full_matrix.reshape(FT // N_ROW, N_ROW, TILE, FT // N_COL, N_COL, TILE)


def draw_child_updates(key, part):
    child_order = CT * TILE
    half_rows = N_ROW // 2
    limit = 0.005
    diagonal = jnp.arange(child_order)[:, None] == jnp.arange(child_order)[None, :]
    blocks = []
    for child in range(2):
        child_key = jax.random.fold_in(key, 17 + child)
        entry_key, pivot_key = jax.random.split(child_key)
        entries = jax.random.uniform(entry_key, (child_order, child_order), jnp.float32, -limit, limit)
        pivots = jax.random.uniform(pivot_key, (child_order,), jnp.float32, -0.5, -0.15)
        symmetric = 0.5 * (entries + entries.T)
        full_matrix = jnp.where(diagonal, pivots[:, None], symmetric)
        blocks.append(full_matrix.reshape(CT // half_rows, half_rows, TILE, CT // N_COL, N_COL, TILE))
    return jnp.stack(blocks, 1).reshape(CT // half_rows, N_ROW, TILE, CT // N_COL, N_COL, TILE)


def draw_child_maps(key, part):
    run_count = CT // RUN
    middle = run_count - 2
    halfway = N_COL // 2
    tile_index = jnp.arange(CT, dtype=jnp.int32)
    first_key, second_key = jax.random.split(jax.random.fold_in(key, 31))
    residues = jax.random.permutation(first_key, 6)[:middle].astype(jnp.int32) + 1
    lifted = residues + 8 * jax.random.randint(second_key, (middle,), 0, 2).astype(jnp.int32)
    offsets_first = jnp.concatenate([jnp.zeros((1,), jnp.int32), jnp.sort(lifted), jnp.full((1,), 15, jnp.int32)])
    third_key, fourth_key = jax.random.split(jax.random.fold_in(key, 32))
    others = jnp.array([value for value in range(2, 7) if value != halfway], jnp.int32)
    picked = jax.random.permutation(third_key, others)[:middle - 2].astype(jnp.int32)
    chosen = jnp.concatenate([jnp.full((1,), halfway, jnp.int32), picked])
    raised = chosen + 8 * jax.random.randint(fourth_key, (middle - 1,), 0, 2).astype(jnp.int32)
    offsets_second = jnp.concatenate([jnp.zeros((1,), jnp.int32), jnp.ones((1,), jnp.int32), jnp.sort(raised), jnp.full((1,), 15, jnp.int32)])
    first_map = tile_index + offsets_first[tile_index // RUN]
    second_map = tile_index + offsets_second[tile_index // RUN]
    return jnp.stack([first_map, second_map]).astype(jnp.int32)


def draw_child_orders(key, part):
    first_key, second_key = jax.random.split(key)
    shortfall = jax.random.randint(first_key, (2,), 0, TILE).astype(jnp.int32)
    full_child = jax.random.randint(second_key, (), 0, 2).astype(jnp.int32)
    shortfall = jnp.where(jnp.arange(2, dtype=jnp.int32) == full_child, 0, shortfall)
    return (CT * TILE - shortfall).astype(jnp.int32)


def setup_inputs(seed: int = 0) -> dict:
    streams_of = jax.random.split(jax.random.key(seed), 5)
    front = draw_front(jax.random.fold_in(streams_of[4], 71), 0)
    child_updates = draw_child_updates(jax.random.fold_in(streams_of[4], 71), 0)
    child_maps = draw_child_maps(jax.random.fold_in(streams_of[4], 71), 0)
    child_orders = draw_child_orders(jax.random.fold_in(streams_of[4], 71), 0)
    return dict(front=front, child_updates=child_updates, child_maps=child_maps, child_orders=child_orders)


def reference(front, child_updates, child_maps, child_orders):
    front_order = FT * TILE
    child_order = CT * TILE
    half_rows = N_ROW // 2
    leading_order = PANELS * PT * TILE
    front_tiles = front.reshape(FT, TILE, FT, TILE).transpose(0, 2, 1, 3)
    children = child_updates.reshape(CT // half_rows, 2, half_rows, TILE, CT // N_COL, N_COL, TILE)
    positions = jnp.arange(child_order, dtype=jnp.int32)
    for child in range(2):
        update = children[:, child].reshape(child_order, child_order)
        inside = (positions < child_orders[child]).astype(jnp.float32)
        update = update * inside[:, None] * inside[None, :]
        update_tiles = update.reshape(CT, TILE, CT, TILE).transpose(0, 2, 1, 3)
        mapping = child_maps[child].astype(jnp.int32)
        front_tiles = front_tiles.at[mapping[:, None], mapping[None, :]].add(update_tiles)
    assembled = front_tiles.transpose(0, 2, 1, 3).reshape(front_order, front_order)
    leading = jnp.tril(jnp.linalg.cholesky(assembled[:leading_order, :leading_order]))
    lower_left = lax.linalg.triangular_solve(leading, assembled[leading_order:, :leading_order], left_side=False, lower=True, transpose_a=True)
    schur = assembled[leading_order:, leading_order:] - jnp.dot(lower_left.astype(jnp.float32), lower_left.T.astype(jnp.float32), precision=lax.Precision.HIGHEST, preferred_element_type=jnp.float32)
    upper_rows = jnp.concatenate([leading, jnp.zeros((leading_order, front_order - leading_order), jnp.float32)], axis=1)
    lower_rows = jnp.concatenate([lower_left, schur], axis=1)
    factored = jnp.concatenate([upper_rows, lower_rows], axis=0)
    return factored.reshape(front.shape)
```

```python
import jax
import jax.numpy as jnp
from jax import lax
from jax.experimental import pallas as pl
from jax.experimental.pallas import tpu as pltpu
from jax.sharding import Mesh
from jax.sharding import PartitionSpec as P

T = 128
PT = 5
ROW_TILES = 6
COL_TILES = 12
CHILD_TILES = 6
ROWS = ("k", "i")
HIGHEST = lax.Precision.HIGHEST
F32 = jnp.float32

VMEM = pl.BlockSpec(memory_space=pltpu.VMEM)
SMEM = pl.BlockSpec(memory_space=pltpu.SMEM)


def shape(*dims):
    return jax.ShapeDtypeStruct(dims, F32)


def params(mib):
    return pltpu.CompilerParams(vmem_limit_bytes=mib * 2**20)


def place():
    return lax.axis_index("k"), lax.axis_index("i"), lax.axis_index("col")


def offset(maps, child, run):
    return maps[child, 8 * run] - 8 * run


def child_tile(child, order, i, j, g, h):
    tile = child[pl.ds(g * T * CHILD_TILES + h, T, stride=CHILD_TILES), :]
    if g == CHILD_TILES - 1:
        rows = lax.broadcasted_iota(jnp.int32, (T, T), 0) + (8 * g + i) * T
        tile = jnp.where(rows < order, tile, 0.0)
    if h == CHILD_TILES - 1:
        cols = lax.broadcasted_iota(jnp.int32, (T, T), 1) + (8 * h + j) * T
        tile = jnp.where(cols < order, tile, 0.0)
    return tile


def pack_panel(maps, orders, front, child, out_rows, out_cols):
    k, i, j = place()
    order = orders[k]
    cols = lax.broadcasted_iota(jnp.int32, (8, T), 1) + (8 * (CHILD_TILES - 1) + j) * T
    for v in range(16):
        for s in range(COL_TILES):
            out_rows[v, s] = front[pl.ds(8 * v * COL_TILES + s, 8, stride=COL_TILES), :]
        for h in range(CHILD_TILES):
            piece = child[pl.ds(8 * v * CHILD_TILES + h, 8, stride=CHILD_TILES), :]
            if h == CHILD_TILES - 1:
                piece = jnp.where(cols < order, piece, 0.0)
            out_rows[v, COL_TILES + h] = piece
    for g in range(CHILD_TILES):
        out_cols[(8 * g + i + offset(maps, k, g)) % 16] = child_tile(child, order, i, j, g, 0)


def pack_main(maps, orders, child, out):
    k, i, j = place()
    order = orders[k]
    for g in range(CHILD_TILES):
        to_i = (i + offset(maps, k, g)) % 8
        for h in range(CHILD_TILES):
            to_j = (j + offset(maps, k, h)) % 8
            out[to_i * 8 + to_j] = child_tile(child, order, i, j, g, h)


def pack_slices(maps, got, out, lead):
    j = lax.axis_index("col")
    for child in range(2):
        for h in range(CHILD_TILES):
            dest = (j + offset(maps, child, h)) % 8
            for b in range(PT):
                out[dest, child, b] = got[8 * child + b, COL_TILES + h]
    for b in range(PT):
        lead[b] = got[b, 0] + got[b, COL_TILES] + got[8 + b, COL_TILES]


def add_slices(maps, got, moved, slab):
    j = lax.axis_index("col")
    for b in range(PT):
        for s in range(COL_TILES):
            slab[b, s] = got[b, s]
    for child in range(2):
        for h in range(CHILD_TILES):
            shift = offset(maps, child, h)
            source = (j - shift) % 8
            s = (8 * h + source + shift) // 8
            for b in range(PT):
                slab[b, s] = slab[b, s] + moved[source, child, b]


def add_column(maps, front, moved, out):
    k, i, j = place()
    row = k * 8 + i
    for t in range(ROW_TILES):
        out[t] = front[pl.ds(t * T * COL_TILES, T, stride=COL_TILES), :]
    for child in range(2):
        for g in range(CHILD_TILES):
            shift = offset(maps, child, g)
            source = (row - 8 * g - shift) % 16

            @pl.when(source < 8)
            def _():
                t = (8 * g + source + shift) // 16
                out[t] = out[t] + moved[8 * child + source]


def invert_factor(lead, out, matrix, work):
    for b in range(PT):
        for c in range(PT):
            for r in range(16):
                matrix[b * T + 8 * r:b * T + 8 * r + 8, c * T:c * T + T] = lead[r * 8 + c, b]
    out[...] = jnp.zeros_like(out)
    sub = lax.broadcasted_iota(jnp.int32, (8, T), 0)
    lane = lax.broadcasted_iota(jnp.int32, (8, T), 1)
    eye = (
        lax.broadcasted_iota(jnp.int32, (T, T), 0) == lax.broadcasted_iota(jnp.int32, (T, T), 1)
    ).astype(F32)
    for b in range(PT):
        lo, hi = b * T, b * T + T
        work[:, :T] = matrix[lo:hi, lo:hi]
        work[:, T:] = eye
        for p in range(16):
            first = 8 * p
            rows = work[first:first + 8, :T]
            other = work[first:first + 8, T:]
            columns = [
                jnp.broadcast_to(rows[:, first + m:first + m + 1], (8, T)) for m in range(8)
            ]
            pivots = jnp.ones((8, T), F32)
            for m in range(8):
                pivot = jnp.broadcast_to(columns[m][m:m + 1, :], (8, T))
                pivots = jnp.where(sub == m, pivot, pivots)
                if m == 7:
                    break
                scale = jnp.where(sub > m, columns[m] * (1.0 / pivot), 0.0)
                rows = rows - scale * rows[m:m + 1, :]
                other = other - scale * other[m:m + 1, :]
                for n in range(m + 1, 8):
                    columns[n] = columns[n] - scale * columns[n][m:m + 1, :]
            out[lo + first:lo + first + 8, lo:hi] = other * lax.rsqrt(pivots)
            if p < 15:
                scaled = jnp.where(lane >= first + 8, rows * (1.0 / pivots), 0.0)
                both = jnp.concatenate([rows, other], axis=1)
                change = lax.dot_general(
                    scaled, both, (((0,), (0,)), ((), ())),
                    precision=HIGHEST, preferred_element_type=F32,
                )
                work[first + 8:, :] = work[first + 8:, :] - change[first + 8:, :]
        inverse = out[lo:hi, lo:hi]
        if b > 0:
            out[lo:hi, :lo] = jnp.dot(
                inverse, out[lo:hi, :lo], precision=HIGHEST, preferred_element_type=F32
            )
        if b < PT - 1:
            right = jnp.dot(
                inverse, matrix[lo:hi, hi:], precision=HIGHEST, preferred_element_type=F32
            )
            matrix[hi:, hi:] = matrix[hi:, hi:] - lax.dot_general(
                right, right, (((0,), (0,)), ((), ())),
                precision=HIGHEST, preferred_element_type=F32,
            )
            out[hi:, :hi] = out[hi:, :hi] - lax.dot_general(
                right, out[lo:hi, :hi], (((0,), (0,)), ((), ())),
                precision=HIGHEST, preferred_element_type=F32,
            )


SPLITS = ((0, 256), (256, 512), (512, 640))


def eliminate(front, across, down, inverse, out, upper, lower, pivot_rows):
    k, i, j = place()
    row = k * 8 + i
    for b in range(PT):
        for r in range(16):
            for s in range(COL_TILES):
                pivot_rows[b * T + 8 * r:b * T + 8 * r + 8, s * T:s * T + T] = across[r, b, s]

    def solve_upper(n, carry):
        part = pl.ds(pl.multiple_of(n * 512, 512), 512)
        for lo, hi in SPLITS:
            upper[lo:hi, part] = jnp.dot(
                inverse[lo:hi, :hi], pivot_rows[:hi, part],
                precision=HIGHEST, preferred_element_type=F32,
            )
        return carry

    lax.fori_loop(0, COL_TILES // 4, solve_upper, 0)

    def solve_lower(t, carry):
        mine = jnp.concatenate([down[b, t] for b in range(PT)], axis=1)
        part = pl.ds(pl.multiple_of(t * T, T), T)
        for lo, hi in SPLITS:
            lower[part, lo:hi] = lax.dot_general(
                mine[:, :hi], inverse[lo:hi, :hi], (((1,), (1,)), ((), ())),
                precision=HIGHEST, preferred_element_type=F32,
            )
        return carry

    lax.fori_loop(0, ROW_TILES, solve_lower, 0)

    def subtract(t, carry):
        part = pl.ds(pl.multiple_of(t * T, T), T)
        for n in range(COL_TILES // 4):
            product = jnp.dot(
                lower[part, :], upper[:, n * 512:n * 512 + 512],
                precision=HIGHEST, preferred_element_type=F32,
            )
            for s in range(4):
                where = pl.ds(t * T * COL_TILES + 4 * n + s, T, stride=COL_TILES)
                out[where, :] = front[where, :] - product[:, s * T:s * T + T]
        return carry

    lax.fori_loop(0, ROW_TILES, subtract, 0)

    x = lax.broadcasted_iota(jnp.int32, (T, T), 0)
    y = lax.broadcasted_iota(jnp.int32, (T, T), 1)

    @pl.when(row < PT)
    def _():
        for s in range(COL_TILES):
            out[pl.ds(s, T, stride=COL_TILES), :] = jnp.zeros((T, T), F32)

    @pl.when(j < PT)
    def _():
        for t in range(ROW_TILES):
            tile = lower[t * T:t * T + T, pl.ds(pl.multiple_of(j * T, T), T)]
            if t == 0:
                tile = jnp.where(row * T + x >= j * T + y, tile, 0.0)
            out[pl.ds(t * T * COL_TILES, T, stride=COL_TILES), :] = tile


def pack_other(maps, moved, out):
    k, i, j = place()
    rank = jnp.int32(0)
    for g in range(CHILD_TILES):
        shift = offset(maps, k, g)
        source = (i - shift) % 8
        leaves = (8 * g + source + shift) // 8 % 2 != k
        here = jnp.minimum(rank, 3)

        @pl.when(leaves)
        def _():
            for h in range(CHILD_TILES):
                out[here, h] = moved[source * 8 + (j - offset(maps, k, h)) % 8]

        rank = rank + leaves.astype(jnp.int32)


def add_children(maps, start, moved, other, out):
    k, i, j = place()
    out[...] = start[...]

    def add(child, g, source, shift, tile_of):
        p = 8 * g + source + shift
        for h in range(CHILD_TILES):
            across = offset(maps, child, h)
            from_j = (j - across) % 8
            q = 8 * h + from_j + across

            @pl.when(jnp.logical_and(p >= PT, q >= PT))
            def _():
                where = pl.ds(p // 16 * (T * COL_TILES) + q // 8, T, stride=COL_TILES)
                out[where, :] = out[where, :] + tile_of(h, from_j)

    rank = jnp.int32(0)
    for g in range(CHILD_TILES):
        shift = offset(maps, k, g)
        source = (i - shift) % 8

        @pl.when((8 * g + source + shift) // 8 % 2 == k)
        def _():
            add(k, g, source, shift, lambda h, from_j: moved[source * 8 + from_j])

        far = 1 - k
        far_shift = offset(maps, far, g)
        far_source = (i - far_shift) % 8
        comes = (8 * g + far_source + far_shift) // 8 % 2 == k
        here = jnp.minimum(rank, 3)

        @pl.when(comes)
        def _():
            add(far, g, far_source, far_shift, lambda h, from_j: other[here, h])

        rank = rank + comes.astype(jnp.int32)


def shards(front, child_updates, child_maps, child_orders):
    front = front.reshape(ROW_TILES * T * COL_TILES, T)
    child = child_updates.reshape(CHILD_TILES * T * CHILD_TILES, T)
    maps = child_maps
    row_slices, column_tiles = pl.pallas_call(
        pack_panel,
        out_shape=(shape(16, 18, 8, T), shape(16, T, T)),
        grid=(1,),
        in_specs=[
            SMEM, SMEM,
            pl.BlockSpec((T * COL_TILES, T), lambda n: (0, 0)),
            pl.BlockSpec((CHILD_TILES * T * CHILD_TILES, T), lambda n: (0, 0)),
        ],
        out_specs=[
            pl.BlockSpec((16, 18, 8, T), lambda n: (0, 0, 0, 0)),
            pl.BlockSpec((16, T, T), lambda n: (0, 0, 0)),
        ],
        compiler_params=params(24),
        name="pack_panel",
    )(maps, child_orders, front, child)
    row_slices = lax.all_to_all(row_slices, ROWS, 0, 0, tiled=True)
    slices, lead = pl.pallas_call(
        pack_slices,
        out_shape=(shape(8, 2, PT, 8, T), shape(PT, 8, T)),
        in_specs=[SMEM, VMEM],
        out_specs=[VMEM, VMEM],
        compiler_params=params(16),
        name="pack_slices",
    )(maps, row_slices)
    lead = lax.all_gather(lead, ("k", "i", "col"))
    slices = lax.all_to_all(slices, "col", 0, 0, tiled=True)
    slab = pl.pallas_call(
        add_slices,
        out_shape=shape(PT, COL_TILES, 8, T),
        in_specs=[SMEM, VMEM, VMEM],
        out_specs=VMEM,
        compiler_params=params(16),
        name="add_slices",
    )(maps, row_slices, slices)
    across = lax.all_gather(slab, ROWS)
    column_tiles = lax.all_to_all(column_tiles, ROWS, 0, 0, tiled=True)
    column = pl.pallas_call(
        add_column,
        out_shape=shape(ROW_TILES, T, T),
        in_specs=[SMEM, VMEM, VMEM],
        out_specs=VMEM,
        compiler_params=params(24),
        name="add_column",
    )(maps, front, column_tiles)
    down = lax.all_gather(column, "col")
    main = pl.pallas_call(
        pack_main,
        out_shape=shape(64, T, T),
        in_specs=[SMEM, SMEM, VMEM],
        out_specs=VMEM,
        compiler_params=params(24),
        name="pack_main",
    )(maps, child_orders, child)
    main = lax.all_to_all(main, ("i", "col"), 0, 0, tiled=True)
    inverse = pl.pallas_call(
        invert_factor,
        out_shape=shape(PT * T, PT * T),
        in_specs=[VMEM],
        out_specs=VMEM,
        scratch_shapes=[pltpu.VMEM((PT * T, PT * T), F32), pltpu.VMEM((T, 2 * T), F32)],
        compiler_params=params(32),
        cost_estimate=pl.CostEstimate(flops=40 * 10**9, bytes_accessed=4 * 2**20, transcendentals=0),
        name="invert_factor",
    )(lead)
    other = pl.pallas_call(
        pack_other,
        out_shape=shape(4, CHILD_TILES, T, T),
        in_specs=[SMEM, VMEM],
        out_specs=VMEM,
        compiler_params=params(24),
        name="pack_other",
    )(maps, main)
    other = lax.ppermute(other, "k", [(0, 1), (1, 0)])
    start = pl.pallas_call(
        eliminate,
        out_shape=shape(ROW_TILES * T * COL_TILES, T),
        in_specs=[VMEM] * 4,
        out_specs=VMEM,
        scratch_shapes=[
            pltpu.VMEM((PT * T, COL_TILES * T), F32),
            pltpu.VMEM((ROW_TILES * T, PT * T), F32),
            pltpu.VMEM((PT * T, COL_TILES * T), F32),
        ],
        compiler_params=params(48),
        cost_estimate=pl.CostEstimate(flops=25 * 10**9, bytes_accessed=20 * 2**20, transcendentals=0),
        name="eliminate",
    )(front, across, down, inverse)
    out = pl.pallas_call(
        add_children,
        out_shape=shape(ROW_TILES * T * COL_TILES, T),
        in_specs=[SMEM, VMEM, VMEM, VMEM],
        out_specs=VMEM,
        compiler_params=params(32),
        name="add_children",
    )(maps, start, main, other)
    return out.reshape(ROW_TILES, 1, T, COL_TILES, 1, T)


def solution(mesh):
    split = Mesh(mesh.devices.reshape(2, 8, 8), ("k", "i", "col"))
    tiles = P(None, ROWS, None, None, "col", None)
    return jax.shard_map(
        shards, mesh=split, in_specs=(tiles, tiles, P(), P()), out_specs=tiles, check_vma=False
    )
```

```python
import jax
import jax.numpy as jnp
from jax import lax
from jax.experimental import pallas as pl
from jax.experimental.pallas import tpu as pltpu
from jax.sharding import Mesh
from jax.sharding import PartitionSpec as P

T = 128
PT = 5
ROW_TILES = 6
COL_TILES = 12
CHILD_TILES = 6
ROWS = ("k", "i")
PIECES = 8 * (COL_TILES + CHILD_TILES)
UPPER = [(b, c) for b in range(PT) for c in range(b, PT)]
HIGHEST = lax.Precision.HIGHEST
F32 = jnp.float32

VMEM = pl.BlockSpec(memory_space=pltpu.VMEM)
SMEM = pl.BlockSpec(memory_space=pltpu.SMEM)


def shape(*dims):
    return jax.ShapeDtypeStruct(dims, F32)


def params(mib):
    return pltpu.CompilerParams(vmem_limit_bytes=mib * 2**20)


def place():
    return lax.axis_index("k"), lax.axis_index("i"), lax.axis_index("col")


def offset(maps, child, run):
    return maps[child, 8 * run] - 8 * run


def child_tile(child, order, i, j, g, h):
    tile = child[pl.ds(g * T * CHILD_TILES + h, T, stride=CHILD_TILES), :]
    if g == CHILD_TILES - 1:
        rows = lax.broadcasted_iota(jnp.int32, (T, T), 0) + (8 * g + i) * T
        tile = jnp.where(rows < order, tile, 0.0)
    if h == CHILD_TILES - 1:
        cols = lax.broadcasted_iota(jnp.int32, (T, T), 1) + (8 * h + j) * T
        tile = jnp.where(cols < order, tile, 0.0)
    return tile


def pack_panel(maps, orders, front, child, out, column):
    k, i, j = place()
    order = orders[k]
    cols = lax.broadcasted_iota(jnp.int32, (8, T), 1) + (8 * (CHILD_TILES - 1) + j) * T
    for v in range(16):
        for s in range(COL_TILES):
            out[v, 8 * s:8 * s + 8] = front[pl.ds(8 * v * COL_TILES + s, 8, stride=COL_TILES), :]
        for h in range(CHILD_TILES):
            piece = child[pl.ds(8 * v * CHILD_TILES + h, 8, stride=CHILD_TILES), :]
            if h == CHILD_TILES - 1:
                piece = jnp.where(cols < order, piece, 0.0)
            s = COL_TILES + h
            out[v, 8 * s:8 * s + 8] = piece
    for g in range(CHILD_TILES):
        tile = child_tile(child, order, i, j, g, 0)
        out[(8 * g + i + offset(maps, k, g)) % 16, PIECES:] = tile
    for t in range(ROW_TILES):
        column[t] = front[pl.ds(t * T * COL_TILES, T, stride=COL_TILES), :]


def pack_main(maps, orders, child, out):
    k, i, j = place()
    order = orders[k]
    for g in range(CHILD_TILES):
        to_i = (i + offset(maps, k, g)) % 8
        for h in range(CHILD_TILES):
            to_j = (j + offset(maps, k, h)) % 8
            out[to_i * 8 + to_j] = child_tile(child, order, i, j, g, h)


def pack_slices(maps, got, out):
    j = lax.axis_index("col")

    def piece(source, s):
        return got[source, 8 * s:8 * s + 8]

    for child in range(2):
        for h in range(CHILD_TILES):
            dest = (j + offset(maps, child, h)) % 8
            for b in range(PT):
                out[dest, child * PT + b] = piece(8 * child + b, COL_TILES + h)
    for b in range(PT):
        lead = piece(b, 0) + piece(b, COL_TILES) + piece(8 + b, COL_TILES)
        for dest in range(8):
            out[dest, 2 * PT + b] = lead


def add_slices(maps, got, moved, slab, lead):
    j = lax.axis_index("col")
    for n, (b, c) in enumerate(UPPER):
        piece = moved[c, 2 * PT + b]
        for v in range(16):
            lead[v, n] = piece
    for b in range(PT):
        for s in range(COL_TILES):
            slab[b, s] = got[b, 8 * s:8 * s + 8]
    for child in range(2):
        for h in range(CHILD_TILES):
            shift = offset(maps, child, h)
            source = (j - shift) % 8
            s = (8 * h + source + shift) // 8
            for b in range(PT):
                slab[b, s] = slab[b, s] + moved[source, child * PT + b]


def add_column(maps, start, moved, out):
    k, i, j = place()
    row = k * 8 + i
    out[...] = start[...]
    for child in range(2):
        for g in range(CHILD_TILES):
            shift = offset(maps, child, g)
            source = (row - 8 * g - shift) % 16

            @pl.when(source < 8)
            def _():
                t = (8 * g + source + shift) // 16
                out[t] = out[t] + moved[8 * child + source, PIECES:]


def invert_factor(lead, out, matrix, work):
    for n, (b, c) in enumerate(UPPER):
        for r in range(16):
            matrix[b * T + 8 * r:b * T + 8 * r + 8, c * T:c * T + T] = lead[r, n]
    out[...] = jnp.zeros_like(out)
    sub = lax.broadcasted_iota(jnp.int32, (8, T), 0)
    lane = lax.broadcasted_iota(jnp.int32, (8, T), 1)
    eye = (
        lax.broadcasted_iota(jnp.int32, (T, T), 0) == lax.broadcasted_iota(jnp.int32, (T, T), 1)
    ).astype(F32)
    for b in range(PT):
        lo, hi = b * T, b * T + T
        work[:, :T] = matrix[lo:hi, lo:hi]
        work[:, T:] = eye
        for p in range(16):
            first = 8 * p
            rows = work[first:first + 8, :T]
            other = work[first:first + 8, T:]
            columns = [
                jnp.broadcast_to(rows[:, first + m:first + m + 1], (8, T)) for m in range(8)
            ]
            pivots = jnp.ones((8, T), F32)
            for m in range(8):
                pivot = jnp.broadcast_to(columns[m][m:m + 1, :], (8, T))
                pivots = jnp.where(sub == m, pivot, pivots)
                if m == 7:
                    break
                scale = jnp.where(sub > m, columns[m] * (1.0 / pivot), 0.0)
                rows = rows - scale * rows[m:m + 1, :]
                other = other - scale * other[m:m + 1, :]
                for n in range(m + 1, 8):
                    columns[n] = columns[n] - scale * columns[n][m:m + 1, :]
            out[lo + first:lo + first + 8, lo:hi] = other * lax.rsqrt(pivots)
            if p < 15:
                scaled = jnp.where(lane >= first + 8, rows * (1.0 / pivots), 0.0)
                both = jnp.concatenate([rows, other], axis=1)
                change = lax.dot_general(
                    scaled, both, (((0,), (0,)), ((), ())),
                    precision=HIGHEST, preferred_element_type=F32,
                )
                work[first + 8:, :] = work[first + 8:, :] - change[first + 8:, :]
        inverse = out[lo:hi, lo:hi]
        if b > 0:
            out[lo:hi, :lo] = jnp.dot(
                inverse, out[lo:hi, :lo], precision=HIGHEST, preferred_element_type=F32
            )
        if b < PT - 1:
            right = jnp.dot(
                inverse, matrix[lo:hi, hi:], precision=HIGHEST, preferred_element_type=F32
            )
            for n in range(b + 1, PT):
                low, high = n * T, n * T + T
                factor = right[:, low - hi:high - hi]
                matrix[low:high, low:] = matrix[low:high, low:] - lax.dot_general(
                    factor, right[:, low - hi:], (((0,), (0,)), ((), ())),
                    precision=HIGHEST, preferred_element_type=F32,
                )
                out[low:high, :hi] = out[low:high, :hi] - lax.dot_general(
                    factor, out[lo:hi, :hi], (((0,), (0,)), ((), ())),
                    precision=HIGHEST, preferred_element_type=F32,
                )


SPLITS = ((0, 256), (256, 512), (512, 640))


def eliminate(front, across, down, inverse, out, upper, lower, pivot_rows):
    k, i, j = place()
    row = k * 8 + i
    for b in range(PT):
        for r in range(16):
            for s in range(COL_TILES):
                pivot_rows[b * T + 8 * r:b * T + 8 * r + 8, s * T:s * T + T] = across[r, b, s]

    def solve_upper(n, carry):
        part = pl.ds(pl.multiple_of(n * 512, 512), 512)
        for lo, hi in SPLITS:
            upper[lo:hi, part] = jnp.dot(
                inverse[lo:hi, :hi], pivot_rows[:hi, part],
                precision=HIGHEST, preferred_element_type=F32,
            )
        return carry

    lax.fori_loop(0, COL_TILES // 4, solve_upper, 0)

    def solve_lower(t, carry):
        mine = jnp.concatenate([down[b, t] for b in range(PT)], axis=1)
        part = pl.ds(pl.multiple_of(t * T, T), T)
        for lo, hi in SPLITS:
            lower[part, lo:hi] = lax.dot_general(
                mine[:, :hi], inverse[lo:hi, :hi], (((1,), (1,)), ((), ())),
                precision=HIGHEST, preferred_element_type=F32,
            )
        return carry

    lax.fori_loop(0, ROW_TILES, solve_lower, 0)

    def subtract(t, carry):
        part = pl.ds(pl.multiple_of(t * T, T), T)
        for n in range(COL_TILES // 4):
            product = jnp.dot(
                lower[part, :], upper[:, n * 512:n * 512 + 512],
                precision=HIGHEST, preferred_element_type=F32,
            )
            for s in range(4):
                where = pl.ds(t * T * COL_TILES + 4 * n + s, T, stride=COL_TILES)
                out[where, :] = front[where, :] - product[:, s * T:s * T + T]
        return carry

    lax.fori_loop(0, ROW_TILES, subtract, 0)

    x = lax.broadcasted_iota(jnp.int32, (T, T), 0)
    y = lax.broadcasted_iota(jnp.int32, (T, T), 1)

    @pl.when(row < PT)
    def _():
        for s in range(COL_TILES):
            out[pl.ds(s, T, stride=COL_TILES), :] = jnp.zeros((T, T), F32)

    @pl.when(j < PT)
    def _():
        for t in range(ROW_TILES):
            tile = lower[t * T:t * T + T, pl.ds(pl.multiple_of(j * T, T), T)]
            if t == 0:
                tile = jnp.where(row * T + x >= j * T + y, tile, 0.0)
            out[pl.ds(t * T * COL_TILES, T, stride=COL_TILES), :] = tile


def pack_other(maps, moved, out):
    k, i, j = place()
    rank = jnp.int32(0)
    for g in range(CHILD_TILES):
        shift = offset(maps, k, g)
        source = (i - shift) % 8
        leaves = (8 * g + source + shift) // 8 % 2 != k
        here = jnp.minimum(rank, 3)

        @pl.when(leaves)
        def _():
            for h in range(CHILD_TILES):
                out[here, h] = moved[source * 8 + (j - offset(maps, k, h)) % 8]

        rank = rank + leaves.astype(jnp.int32)


def add_children(maps, start, moved, other, out):
    k, i, j = place()
    t = pl.program_id(0)
    out[...] = start[...]

    def add(child, p, tile_of):
        for h in range(CHILD_TILES):
            across = offset(maps, child, h)
            from_j = (j - across) % 8
            q = 8 * h + from_j + across

            @pl.when(q >= PT)
            def _():
                where = pl.ds(q // 8, T, stride=COL_TILES)
                out[where, :] = out[where, :] + tile_of(h, from_j)

    rank = jnp.int32(0)
    for g in range(CHILD_TILES):
        shift = offset(maps, k, g)
        source = (i - shift) % 8
        p = 8 * g + source + shift
        mine = jnp.logical_and(p // 8 % 2 == k, p >= PT)

        @pl.when(jnp.logical_and(mine, p // 16 == t))
        def _():
            add(k, p, lambda h, from_j: moved[source * 8 + from_j])

        far = 1 - k
        far_shift = offset(maps, far, g)
        far_p = 8 * g + (i - far_shift) % 8 + far_shift
        comes = far_p // 8 % 2 == k
        here = jnp.minimum(rank, 3)

        @pl.when(jnp.logical_and(jnp.logical_and(comes, far_p >= PT), far_p // 16 == t))
        def _():
            add(far, far_p, lambda h, from_j: other[here, h])

        rank = rank + comes.astype(jnp.int32)


def shards(front, child_updates, child_maps, child_orders):
    front = front.reshape(ROW_TILES * T * COL_TILES, T)
    child = child_updates.reshape(CHILD_TILES * T * CHILD_TILES, T)
    maps = child_maps
    panel, column = pl.pallas_call(
        pack_panel,
        out_shape=(shape(16, PIECES + T, T), shape(ROW_TILES, T, T)),
        in_specs=[SMEM, SMEM, VMEM, VMEM],
        out_specs=[VMEM, VMEM],
        compiler_params=params(24),
        name="pack_panel",
    )(maps, child_orders, front, child)
    panel = lax.all_to_all(panel, ROWS, 0, 0, tiled=True)
    slices = pl.pallas_call(
        pack_slices,
        out_shape=shape(8, 3 * PT, 8, T),
        in_specs=[SMEM, VMEM],
        out_specs=VMEM,
        compiler_params=params(16),
        name="pack_slices",
    )(maps, panel)
    slices = lax.all_to_all(slices, "col", 0, 0, tiled=True)
    column = pl.pallas_call(
        add_column,
        out_shape=shape(ROW_TILES, T, T),
        in_specs=[SMEM, VMEM, VMEM],
        out_specs=VMEM,
        compiler_params=params(24),
        name="add_column",
    )(maps, column, panel)
    down = lax.all_gather(column, "col")
    slab, lead = pl.pallas_call(
        add_slices,
        out_shape=(shape(PT, COL_TILES, 8, T), shape(16, len(UPPER), 8, T)),
        in_specs=[SMEM, VMEM, VMEM],
        out_specs=[VMEM, VMEM],
        compiler_params=params(16),
        name="add_slices",
    )(maps, panel, slices)
    across = lax.all_gather(slab, ROWS)
    lead = lax.all_to_all(lead, ROWS, 0, 0, tiled=True)
    main = pl.pallas_call(
        pack_main,
        out_shape=shape(64, T, T),
        in_specs=[SMEM, SMEM, VMEM],
        out_specs=VMEM,
        compiler_params=params(24),
        name="pack_main",
    )(maps, child_orders, child)
    main = lax.all_to_all(main, ("i", "col"), 0, 0, tiled=True)
    inverse = pl.pallas_call(
        invert_factor,
        out_shape=shape(PT * T, PT * T),
        in_specs=[VMEM],
        out_specs=VMEM,
        scratch_shapes=[pltpu.VMEM((PT * T, PT * T), F32), pltpu.VMEM((T, 2 * T), F32)],
        compiler_params=params(32),
        cost_estimate=pl.CostEstimate(flops=40 * 10**9, bytes_accessed=4 * 2**20, transcendentals=0),
        name="invert_factor",
    )(lead)
    other = pl.pallas_call(
        pack_other,
        out_shape=shape(4, CHILD_TILES, T, T),
        in_specs=[SMEM, VMEM],
        out_specs=VMEM,
        compiler_params=params(24),
        name="pack_other",
    )(maps, main)
    other = lax.ppermute(other, "k", [(0, 1), (1, 0)])
    start = pl.pallas_call(
        eliminate,
        out_shape=shape(ROW_TILES * T * COL_TILES, T),
        in_specs=[VMEM] * 4,
        out_specs=VMEM,
        scratch_shapes=[
            pltpu.VMEM((PT * T, COL_TILES * T), F32),
            pltpu.VMEM((ROW_TILES * T, PT * T), F32),
            pltpu.VMEM((PT * T, COL_TILES * T), F32),
        ],
        compiler_params=params(48),
        cost_estimate=pl.CostEstimate(flops=25 * 10**9, bytes_accessed=20 * 2**20, transcendentals=0),
        name="eliminate",
    )(front, across, down, inverse)
    block = pl.BlockSpec((T * COL_TILES, T), lambda t: (t, 0))
    out = pl.pallas_call(
        add_children,
        out_shape=shape(ROW_TILES * T * COL_TILES, T),
        grid=(4,),
        in_specs=[SMEM, block, VMEM, VMEM],
        out_specs=block,
        input_output_aliases={1: 0},
        compiler_params=params(32),
        name="add_children",
    )(maps, start, main, other)
    return out.reshape(ROW_TILES, 1, T, COL_TILES, 1, T)


def solution(mesh):
    split = Mesh(mesh.devices.reshape(2, 8, 8), ("k", "i", "col"))
    tiles = P(None, ROWS, None, None, "col", None)
    return jax.shard_map(
        shards, mesh=split, in_specs=(tiles, tiles, P(), P()), out_specs=tiles, check_vma=False
    )
```

```python
import jax
import jax.numpy as jnp
from jax import lax
from jax.experimental import pallas as pl
from jax.experimental.pallas import tpu as pltpu
from jax.sharding import Mesh
from jax.sharding import PartitionSpec as P

T = 128
PT = 5
ROW_TILES = 6
COL_TILES = 12
CHILD_TILES = 6
ROWS = ("k", "i")
PIECES = 8 * (COL_TILES + CHILD_TILES)
UPPER = [(b, c) for b in range(PT) for c in range(b, PT)]
GROUP = 32
HIGHEST = lax.Precision.HIGHEST
F32 = jnp.float32
BF16 = jnp.bfloat16

VMEM = pl.BlockSpec(memory_space=pltpu.VMEM)
SMEM = pl.BlockSpec(memory_space=pltpu.SMEM)


def shape(*dims):
    return jax.ShapeDtypeStruct(dims, F32)


def params(mib):
    return pltpu.CompilerParams(vmem_limit_bytes=mib * 2**20)


def place():
    return lax.axis_index("k"), lax.axis_index("i"), lax.axis_index("col")


def offset(maps, child, run):
    return maps[child, 8 * run] - 8 * run


def child_tile(child, order, i, j, g, h):
    tile = child[pl.ds(g * T * CHILD_TILES + h, T, stride=CHILD_TILES), :]
    if g == CHILD_TILES - 1:
        rows = lax.broadcasted_iota(jnp.int32, (T, T), 0) + (8 * g + i) * T
        tile = jnp.where(rows < order, tile, 0.0)
    if h == CHILD_TILES - 1:
        cols = lax.broadcasted_iota(jnp.int32, (T, T), 1) + (8 * h + j) * T
        tile = jnp.where(cols < order, tile, 0.0)
    return tile


def pack_panel(maps, orders, front, child, out, column):
    k, i, j = place()
    order = orders[k]
    cols = lax.broadcasted_iota(jnp.int32, (8, T), 1) + (8 * (CHILD_TILES - 1) + j) * T
    for v in range(16):
        for s in range(COL_TILES):
            out[v, 8 * s:8 * s + 8] = front[pl.ds(8 * v * COL_TILES + s, 8, stride=COL_TILES), :]
        for h in range(CHILD_TILES):
            piece = child[pl.ds(8 * v * CHILD_TILES + h, 8, stride=CHILD_TILES), :]
            if h == CHILD_TILES - 1:
                piece = jnp.where(cols < order, piece, 0.0)
            s = COL_TILES + h
            out[v, 8 * s:8 * s + 8] = piece
    for g in range(CHILD_TILES):
        tile = child_tile(child, order, i, j, g, 0)
        out[(8 * g + i + offset(maps, k, g)) % 16, PIECES:] = tile
    for t in range(ROW_TILES):
        column[t] = front[pl.ds(t * T * COL_TILES, T, stride=COL_TILES), :]


def pack_main(maps, orders, child, out):
    k, i, j = place()
    order = orders[k]
    for g in range(CHILD_TILES):
        to_i = (i + offset(maps, k, g)) % 8
        for h in range(CHILD_TILES):
            to_j = (j + offset(maps, k, h)) % 8
            out[to_i * 8 + to_j] = child_tile(child, order, i, j, g, h)


def pack_slices(maps, orders, got, child, out, main):
    j = lax.axis_index("col")

    pack_main(maps, orders, child, main)

    def piece(source, s):
        return got[source, 8 * s:8 * s + 8]

    for child in range(2):
        for h in range(CHILD_TILES):
            dest = (j + offset(maps, child, h)) % 8
            for b in range(PT):
                out[dest, child * PT + b] = piece(8 * child + b, COL_TILES + h)
    for b in range(PT):
        lead = piece(b, 0) + piece(b, COL_TILES) + piece(8 + b, COL_TILES)
        for dest in range(8):
            out[dest, 2 * PT + b] = lead


def add_slices(maps, got, moved, slab):
    j = lax.axis_index("col")
    for b in range(PT):
        for s in range(COL_TILES):
            slab[b, s] = got[b, 8 * s:8 * s + 8]
    for child in range(2):
        for h in range(CHILD_TILES):
            shift = offset(maps, child, h)
            source = (j - shift) % 8
            s = (8 * h + source + shift) // 8
            for b in range(PT):
                slab[b, s] = slab[b, s] + moved[source, child * PT + b]


def add_column(maps, start, moved, out):
    k, i, j = place()
    row = k * 8 + i
    out[...] = start[...]
    for child in range(2):
        for g in range(CHILD_TILES):
            shift = offset(maps, child, g)
            source = (row - 8 * g - shift) % 16

            @pl.when(source < 8)
            def _():
                t = (8 * g + source + shift) // 16
                out[t] = out[t] + moved[8 * child + source, PIECES:]


def reciprocal(x):
    y = pl.reciprocal(x, approx=True)
    y = y * (2.0 - x * y)
    return y * (2.0 - x * y)


def invert_factor(lead, out, matrix, work):
    for n, (b, c) in enumerate(UPPER):
        for r in range(16):
            matrix[b * T + 8 * r:b * T + 8 * r + 8, c * T:c * T + T] = lead[r, n]
    out[...] = jnp.zeros_like(out)
    sub = lax.broadcasted_iota(jnp.int32, (8, T), 0)
    eye = (
        lax.broadcasted_iota(jnp.int32, (T, T), 0) == lax.broadcasted_iota(jnp.int32, (T, T), 1)
    ).astype(F32)
    for b in range(PT):
        lo, hi = b * T, b * T + T
        work[:, :T] = matrix[lo:hi, lo:hi]
        work[:, T:] = eye
        for base in range(0, T, GROUP):
            rows = [work[base + 8 * q:base + 8 * q + 8, :T] for q in range(GROUP // 8)]
            other = [work[base + 8 * q:base + 8 * q + 8, T:] for q in range(GROUP // 8)]
            inverses = []
            for p in range(GROUP // 8):
                first = base + 8 * p
                after = range(p, GROUP // 8)
                columns = {
                    q: [
                        jnp.broadcast_to(rows[q][:, first + m:first + m + 1], (8, T))
                        for m in range(8)
                    ]
                    for q in after
                }
                pivots = jnp.ones((8, T), F32)
                for m in range(8):
                    pivot = jnp.broadcast_to(columns[p][m][m:m + 1, :], (8, T))
                    pivots = jnp.where(sub == m, pivot, pivots)
                    over = reciprocal(pivot)
                    row = jnp.broadcast_to(rows[p][m:m + 1, :], (8, T))
                    mate = jnp.broadcast_to(other[p][m:m + 1, :], (8, T))
                    for n in range(m + 1, 8):
                        head = jnp.broadcast_to(columns[p][n][m:m + 1, :], (8, T))
                        for q in after:
                            scale = columns[q][m] * over
                            if q == p:
                                scale = jnp.where(sub > m, scale, 0.0)
                            columns[q][n] = columns[q][n] - scale * head
                    for q in after:
                        scale = columns[q][m] * over
                        if q == p:
                            if m == 7:
                                continue
                            scale = jnp.where(sub > m, scale, 0.0)
                        rows[q] = rows[q] - scale * row
                        other[q] = other[q] - scale * mate
                out[lo + first:lo + first + 8, lo:hi] = other[p] * lax.rsqrt(pivots)
                inverses.append(1.0 / pivots)
            if base + GROUP < T:
                scaled = jnp.concatenate([x * y for x, y in zip(rows, inverses)], axis=0)
                both = jnp.concatenate(
                    [jnp.concatenate(rows, axis=0), jnp.concatenate(other, axis=0)], axis=1
                )
                change = jnp.dot(
                    scaled.T[base + GROUP:, :], both,
                    precision=HIGHEST, preferred_element_type=F32,
                )
                work[base + GROUP:, :] = work[base + GROUP:, :] - change
        inverse = out[lo:hi, lo:hi]
        if b > 0:
            out[lo:hi, :lo] = jnp.dot(
                inverse, out[lo:hi, :lo], precision=HIGHEST, preferred_element_type=F32
            )
        if b < PT - 1:
            right = jnp.dot(
                inverse, matrix[lo:hi, hi:], precision=HIGHEST, preferred_element_type=F32
            )
            for n in range(b + 1, PT):
                low, high = n * T, n * T + T
                factor = right[:, low - hi:high - hi]
                matrix[low:high, low:] = matrix[low:high, low:] - lax.dot_general(
                    factor, right[:, low - hi:], (((0,), (0,)), ((), ())),
                    precision=HIGHEST, preferred_element_type=F32,
                )
                out[low:high, :hi] = out[low:high, :hi] - lax.dot_general(
                    factor, out[lo:hi, :hi], (((0,), (0,)), ((), ())),
                    precision=HIGHEST, preferred_element_type=F32,
                )


SPLITS = ((0, 256), (256, 512), (512, 640))
WIDE = 512


def halves(x):
    high = x.astype(BF16)
    return high, (x - high.astype(F32)).astype(BF16)


def product(a, b):
    (a_high, a_low), (b_high, b_low) = a, b
    small = jnp.dot(a_high, b_low, preferred_element_type=F32) + jnp.dot(
        a_low, b_high, preferred_element_type=F32
    )
    return jnp.dot(a_high, b_high, preferred_element_type=F32) + small


def eliminate(
    maps, front, across, down, inverse, moved, other, out,
    pivot_high, pivot_low, inverse_high, inverse_low, upper_high, upper_low, lower,
):
    k, i, j = place()
    row = k * 8 + i
    t = pl.program_id(0)

    @pl.when(t == 0)
    def _():
        for b in range(PT):
            for s in range(COL_TILES):
                tile = across[:, b, s].reshape(T, T)
                high, low = halves(tile)
                pivot_high[b * T:b * T + T, s * T:s * T + T] = high
                pivot_low[b * T:b * T + T, s * T:s * T + T] = low
        high, low = halves(inverse[...])
        inverse_high[...] = high
        inverse_low[...] = low

        def solve_upper(n, carry):
            part = pl.ds(pl.multiple_of(n * WIDE, WIDE), WIDE)
            for lo, hi in SPLITS:
                high, low = halves(product(
                    (inverse_high[lo:hi, :hi], inverse_low[lo:hi, :hi]),
                    (pivot_high[:hi, part], pivot_low[:hi, part]),
                ))
                upper_high[lo:hi, part] = high
                upper_low[lo:hi, part] = low
            return carry

        lax.fori_loop(0, COL_TILES * T // WIDE, solve_upper, 0)

        def solve_lower(t, carry):
            mine = jnp.concatenate([down[b, t] for b in range(PT)], axis=1)
            part = pl.ds(pl.multiple_of(t * T, T), T)
            for lo, hi in SPLITS:
                lower[part, lo:hi] = lax.dot_general(
                    mine[:, :hi], inverse[lo:hi, :hi], (((1,), (1,)), ((), ())),
                    precision=HIGHEST, preferred_element_type=F32,
                )
            return carry

        lax.fori_loop(0, ROW_TILES, solve_lower, 0)

    mine = lower[pl.ds(pl.multiple_of(t * T, T), T), :]
    mine_halves = halves(mine)
    for n in range(COL_TILES * T // WIDE):
        change = product(
            mine_halves,
            (upper_high[:, n * WIDE:n * WIDE + WIDE], upper_low[:, n * WIDE:n * WIDE + WIDE]),
        )
        for s in range(WIDE // T):
            where = pl.ds(n * (WIDE // T) + s, T, stride=COL_TILES)
            out[where, :] = front[where, :] - change[:, s * T:s * T + T]

    add_children(maps, moved, other, out)
    first = jnp.logical_and(t == 0, row < PT)

    @pl.when(first)
    def _():
        for s in range(COL_TILES):
            out[pl.ds(s, T, stride=COL_TILES), :] = jnp.zeros((T, T), F32)

    @pl.when(j < PT)
    def _():
        part = pl.ds(pl.multiple_of(t * T, T), T)
        tile = lower[part, pl.ds(pl.multiple_of(j * T, T), T)]
        x = lax.broadcasted_iota(jnp.int32, (T, T), 0) + (16 * t + row) * T
        y = lax.broadcasted_iota(jnp.int32, (T, T), 1) + j * T
        out[pl.ds(0, T, stride=COL_TILES), :] = jnp.where(x >= y, tile, 0.0)


def pack_other(maps, moved, slices, out, lead):
    k, i, j = place()
    for n, (b, c) in enumerate(UPPER):
        piece = slices[c, 2 * PT + b]
        for v in range(16):
            lead[v, n] = piece
    rank = jnp.int32(0)
    for g in range(CHILD_TILES):
        shift = offset(maps, k, g)
        source = (i - shift) % 8
        leaves = (8 * g + source + shift) // 8 % 2 != k
        here = jnp.minimum(rank, 3)

        @pl.when(leaves)
        def _():
            for h in range(CHILD_TILES):
                out[here, h] = moved[source * 8 + (j - offset(maps, k, h)) % 8]

        rank = rank + leaves.astype(jnp.int32)


def add_children(maps, moved, other, out):
    k, i, j = place()
    t = pl.program_id(0)

    def add(child, tile_of):
        for h in range(CHILD_TILES):
            across = offset(maps, child, h)
            from_j = (j - across) % 8
            where = pl.ds((8 * h + from_j + across) // 8, T, stride=COL_TILES)
            out[where, :] = out[where, :] + tile_of(h, from_j)

    rank = jnp.int32(0)
    for g in range(CHILD_TILES):
        shift = offset(maps, k, g)
        source = (i - shift) % 8
        p = 8 * g + source + shift
        mine = p // 8 % 2 == k

        @pl.when(jnp.logical_and(mine, p // 16 == t))
        def _():
            add(k, lambda h, from_j: moved[source * 8 + from_j])

        far = 1 - k
        far_shift = offset(maps, far, g)
        far_p = 8 * g + (i - far_shift) % 8 + far_shift
        comes = far_p // 8 % 2 == k
        here = jnp.minimum(rank, 3)

        @pl.when(jnp.logical_and(comes, far_p // 16 == t))
        def _():
            add(far, lambda h, from_j: other[here, h])

        rank = rank + comes.astype(jnp.int32)


def shards(front, child_updates, child_maps, child_orders):
    front = front.reshape(ROW_TILES * T * COL_TILES, T)
    child = child_updates.reshape(CHILD_TILES * T * CHILD_TILES, T)
    maps = child_maps
    panel, column = pl.pallas_call(
        pack_panel,
        out_shape=(shape(16, PIECES + T, T), shape(ROW_TILES, T, T)),
        in_specs=[SMEM, SMEM, VMEM, VMEM],
        out_specs=[VMEM, VMEM],
        compiler_params=params(24),
        name="pack_panel",
    )(maps, child_orders, front, child)
    panel = lax.all_to_all(panel, ROWS, 0, 0, tiled=True)
    slices, main = pl.pallas_call(
        pack_slices,
        out_shape=(shape(8, 3 * PT, 8, T), shape(64, T, T)),
        in_specs=[SMEM, SMEM, VMEM, VMEM],
        out_specs=[VMEM, VMEM],
        compiler_params=params(24),
        name="pack_slices",
    )(maps, child_orders, panel, child)
    slices = lax.all_to_all(slices, "col", 0, 0, tiled=True)
    column = pl.pallas_call(
        add_column,
        out_shape=shape(ROW_TILES, T, T),
        in_specs=[SMEM, VMEM, VMEM],
        out_specs=VMEM,
        compiler_params=params(24),
        name="add_column",
    )(maps, column, panel)
    down = lax.all_gather(column, "col")
    slab = pl.pallas_call(
        add_slices,
        out_shape=shape(PT, COL_TILES, 8, T),
        in_specs=[SMEM, VMEM, VMEM],
        out_specs=VMEM,
        compiler_params=params(16),
        name="add_slices",
    )(maps, panel, slices)
    across = lax.all_gather(slab, ROWS)
    main = lax.all_to_all(main, ("i", "col"), 0, 0, tiled=True)
    other, lead = pl.pallas_call(
        pack_other,
        out_shape=(shape(4, CHILD_TILES, T, T), shape(16, len(UPPER), 8, T)),
        in_specs=[SMEM, VMEM, VMEM],
        out_specs=[VMEM, VMEM],
        compiler_params=params(24),
        name="pack_other",
    )(maps, main, slices)
    lead = lax.all_to_all(lead, ROWS, 0, 0, tiled=True)
    other = lax.ppermute(other, "k", [(0, 1), (1, 0)])
    inverse = pl.pallas_call(
        invert_factor,
        out_shape=shape(PT * T, PT * T),
        in_specs=[VMEM],
        out_specs=VMEM,
        scratch_shapes=[pltpu.VMEM((PT * T, PT * T), F32), pltpu.VMEM((T, 2 * T), F32)],
        compiler_params=params(32),
        cost_estimate=pl.CostEstimate(flops=40 * 10**9, bytes_accessed=4 * 2**20, transcendentals=0),
        name="invert_factor",
    )(lead)
    block = pl.BlockSpec((T * COL_TILES, T), lambda t: (t, 0))
    out = pl.pallas_call(
        eliminate,
        out_shape=shape(ROW_TILES * T * COL_TILES, T),
        grid=(ROW_TILES,),
        in_specs=[SMEM, block] + [VMEM] * 5,
        out_specs=block,
        scratch_shapes=[
            pltpu.VMEM((PT * T, COL_TILES * T), BF16),
            pltpu.VMEM((PT * T, COL_TILES * T), BF16),
            pltpu.VMEM((PT * T, PT * T), BF16),
            pltpu.VMEM((PT * T, PT * T), BF16),
            pltpu.VMEM((PT * T, COL_TILES * T), BF16),
            pltpu.VMEM((PT * T, COL_TILES * T), BF16),
            pltpu.VMEM((ROW_TILES * T, PT * T), F32),
        ],
        compiler_params=params(40),
        cost_estimate=pl.CostEstimate(flops=15 * 10**9, bytes_accessed=20 * 2**20, transcendentals=0),
        name="eliminate",
    )(maps, front, across, down, inverse, main, other)
    return out.reshape(ROW_TILES, 1, T, COL_TILES, 1, T)


def solution(mesh):
    split = Mesh(mesh.devices.reshape(2, 8, 8), ("k", "i", "col"))
    tiles = P(None, ROWS, None, None, "col", None)
    return jax.shard_map(
        shards, mesh=split, in_specs=(tiles, tiles, P(), P()), out_specs=tiles, check_vma=False
    )
```

```python
import jax
import jax.numpy as jnp
from jax import lax
from jax.experimental import pallas as pl
from jax.experimental.pallas import tpu as pltpu
from jax.sharding import Mesh
from jax.sharding import PartitionSpec as P

T = 128
PT = 5
ROW_TILES = 6
COL_TILES = 12
CHILD_TILES = 6
ROWS = ("k", "i")
PIECES = COL_TILES + CHILD_TILES
UPPER = [(b, c) for b in range(PT) for c in range(b, PT)]
GROUP = 32
HIGHEST = lax.Precision.HIGHEST
F32 = jnp.float32
BF16 = jnp.bfloat16

VMEM = pl.BlockSpec(memory_space=pltpu.VMEM)
ANY = pl.BlockSpec(memory_space=pl.ANY)
SMEM = pl.BlockSpec(memory_space=pltpu.SMEM)


def shape(*dims):
    return jax.ShapeDtypeStruct(dims, F32)


def params(mib):
    return pltpu.CompilerParams(vmem_limit_bytes=mib * 2**20)


def place():
    return lax.axis_index("k"), lax.axis_index("i"), lax.axis_index("col")


def offset(maps, child, run):
    return maps[child, 8 * run] - 8 * run


def child_tile(child, order, i, j, g, h):
    tile = child[pl.ds(g * T * CHILD_TILES + h, T, stride=CHILD_TILES), :]
    if g == CHILD_TILES - 1:
        rows = lax.broadcasted_iota(jnp.int32, (T, T), 0) + (8 * g + i) * T
        tile = jnp.where(rows < order, tile, 0.0)
    if h == CHILD_TILES - 1:
        cols = lax.broadcasted_iota(jnp.int32, (T, T), 1) + (8 * h + j) * T
        tile = jnp.where(cols < order, tile, 0.0)
    return tile


def pack_panel(maps, orders, front, child, moved, out, column):
    k, i, j = place()
    order = orders[k]
    cols = lax.broadcasted_iota(jnp.int32, (8, T), 1) + (8 * (CHILD_TILES - 1) + j) * T
    for v in range(16):
        for s in range(COL_TILES):
            out[v, s] = front[pl.ds(8 * v * COL_TILES + s, 8, stride=COL_TILES), :]
        for h in range(CHILD_TILES):
            piece = child[pl.ds(8 * v * CHILD_TILES + h, 8, stride=CHILD_TILES), :]
            if h == CHILD_TILES - 1:
                piece = jnp.where(cols < order, piece, 0.0)
            out[v, COL_TILES + h] = piece
    row = k * 8 + i
    for t in range(ROW_TILES):
        column[t] = front[pl.ds(t * T * COL_TILES, T, stride=COL_TILES), :]
    for source_child in range(2):
        for g in range(CHILD_TILES):
            shift = offset(maps, source_child, g)
            source = (row - 8 * g - shift) % 16

            @pl.when(source < 8)
            def _():
                t = (8 * g + source + shift) // 16
                column[t] = column[t] + moved[8 * source_child + source]


def pack_main(maps, orders, child, out):
    k, i, j = place()
    order = orders[k]
    for g in range(CHILD_TILES):
        to_i = (i + offset(maps, k, g)) % 8
        for h in range(CHILD_TILES):
            to_j = (j + offset(maps, k, h)) % 8
            out[to_i * 8 + to_j] = child_tile(child, order, i, j, g, h)


def pack_slices(maps, got, out):
    j = lax.axis_index("col")
    for child in range(2):
        for h in range(CHILD_TILES):
            dest = (j + offset(maps, child, h)) % 8
            for b in range(PT):
                out[dest, child * PT + b] = got[8 * child + b, COL_TILES + h]
    for b in range(PT):
        lead = got[b, 0] + got[b, COL_TILES] + got[8 + b, COL_TILES]
        for dest in range(8):
            out[dest, 2 * PT + b] = lead


def add_slices(maps, got, moved, other, slab, lead):
    j = lax.axis_index("col")
    for n, (b, c) in enumerate(UPPER):
        piece = moved[c, 2 * PT + b]
        for v in range(16):
            lead[v, n] = piece
    for b in range(PT):
        for s in range(COL_TILES):
            slab[b, s] = got[b, s]
    for child in range(2):
        for h in range(CHILD_TILES):
            shift = offset(maps, child, h)
            source = (j - shift) % 8
            s = (8 * h + source + shift) // 8
            for b in range(PT):
                slab[b, s] = slab[b, s] + moved[source, child * PT + b]


def reciprocal(x):
    y = pl.reciprocal(x, approx=True)
    y = y * (2.0 - x * y)
    return y * (2.0 - x * y)


def invert_factor(lead, out, matrix, work):
    for n, (b, c) in enumerate(UPPER):
        for r in range(16):
            matrix[b * T + 8 * r:b * T + 8 * r + 8, c * T:c * T + T] = lead[r, n]
    out[...] = jnp.zeros_like(out)
    sub = lax.broadcasted_iota(jnp.int32, (8, T), 0)
    eye = (
        lax.broadcasted_iota(jnp.int32, (T, T), 0) == lax.broadcasted_iota(jnp.int32, (T, T), 1)
    ).astype(F32)
    for b in range(PT):
        lo, hi = b * T, b * T + T
        work[:, :T] = matrix[lo:hi, lo:hi]
        work[:, T:] = eye
        for base in range(0, T, GROUP):
            rows = [work[base + 8 * q:base + 8 * q + 8, :T] for q in range(GROUP // 8)]
            other = [work[base + 8 * q:base + 8 * q + 8, T:] for q in range(GROUP // 8)]
            inverses = []
            for p in range(GROUP // 8):
                first = base + 8 * p
                after = range(p, GROUP // 8)
                columns = {
                    q: [
                        jnp.broadcast_to(rows[q][:, first + m:first + m + 1], (8, T))
                        for m in range(8)
                    ]
                    for q in after
                }
                pivots = jnp.ones((8, T), F32)
                for m in range(8):
                    pivot = jnp.broadcast_to(columns[p][m][m:m + 1, :], (8, T))
                    pivots = jnp.where(sub == m, pivot, pivots)
                    over = reciprocal(pivot)
                    row = jnp.broadcast_to(rows[p][m:m + 1, :], (8, T))
                    mate = jnp.broadcast_to(other[p][m:m + 1, :], (8, T))
                    for n in range(m + 1, 8):
                        head = jnp.broadcast_to(columns[p][n][m:m + 1, :], (8, T))
                        for q in after:
                            scale = columns[q][m] * over
                            if q == p:
                                scale = jnp.where(sub > m, scale, 0.0)
                            columns[q][n] = columns[q][n] - scale * head
                    for q in after:
                        scale = columns[q][m] * over
                        if q == p:
                            if m == 7:
                                continue
                            scale = jnp.where(sub > m, scale, 0.0)
                        rows[q] = rows[q] - scale * row
                        other[q] = other[q] - scale * mate
                out[lo + first:lo + first + 8, lo:hi] = other[p] * lax.rsqrt(pivots)
                inverses.append(1.0 / pivots)
            if base + GROUP < T:
                scaled = jnp.concatenate([x * y for x, y in zip(rows, inverses)], axis=0)
                both = jnp.concatenate(
                    [jnp.concatenate(rows, axis=0), jnp.concatenate(other, axis=0)], axis=1
                )
                change = jnp.dot(
                    scaled.T[base + GROUP:, :], both,
                    precision=HIGHEST, preferred_element_type=F32,
                )
                work[base + GROUP:, :] = work[base + GROUP:, :] - change
        inverse = out[lo:hi, lo:hi]
        if b > 0:
            out[lo:hi, :lo] = jnp.dot(
                inverse, out[lo:hi, :lo], precision=HIGHEST, preferred_element_type=F32
            )
        if b < PT - 1:
            right = jnp.dot(
                inverse, matrix[lo:hi, hi:], precision=HIGHEST, preferred_element_type=F32
            )
            for n in range(b + 1, PT):
                low, high = n * T, n * T + T
                factor = right[:, low - hi:high - hi]
                matrix[low:high, low:] = matrix[low:high, low:] - lax.dot_general(
                    factor, right[:, low - hi:], (((0,), (0,)), ((), ())),
                    precision=HIGHEST, preferred_element_type=F32,
                )
                out[low:high, :hi] = out[low:high, :hi] - lax.dot_general(
                    factor, out[lo:hi, :hi], (((0,), (0,)), ((), ())),
                    precision=HIGHEST, preferred_element_type=F32,
                )


SPLITS = ((0, 256), (256, 512), (512, 640))
WIDE = 512


def halves(x):
    high = x.astype(BF16)
    return high, (x - high.astype(F32)).astype(BF16)


def product(a, b):
    (a_high, a_low), (b_high, b_low) = a, b
    small = jnp.dot(a_high, b_low, preferred_element_type=F32) + jnp.dot(
        a_low, b_high, preferred_element_type=F32
    )
    return jnp.dot(a_high, b_high, preferred_element_type=F32) + small


def solve_rows(down, inverse, lower, inverse_high, inverse_low):
    high, low = halves(inverse[...])
    inverse_high[...] = high
    inverse_low[...] = low

    def solve(t, carry):
        mine = jnp.concatenate([down[b, t] for b in range(PT)], axis=1)
        part = pl.ds(pl.multiple_of(t * T, T), T)
        for lo, hi in SPLITS:
            lower[part, lo:hi] = lax.dot_general(
                mine[:, :hi], inverse[lo:hi, :hi], (((1,), (1,)), ((), ())),
                precision=HIGHEST, preferred_element_type=F32,
            )
        return carry

    lax.fori_loop(0, ROW_TILES, solve, 0)


def eliminate(
    maps, front, across_far, lower, inverse_high, inverse_low, moved_far, other_far, out,
    pivot_high, pivot_low, upper_high, upper_low, across, moved, other, across_sem, sems,
):
    k, i, j = place()
    row = k * 8 + i
    t = pl.program_id(0)

    def child_copies():
        return (
            pltpu.make_async_copy(moved_far, moved, sems.at[0]),
            pltpu.make_async_copy(other_far, other, sems.at[1]),
        )

    @pl.when(t == 0)
    def _():
        arrivals = [
            pltpu.make_async_copy(across_far.at[:, b], across.at[:, b], across_sem.at[b])
            for b in range(PT)
        ]
        for copy in (*arrivals, *child_copies()):
            copy.start()
        for b in range(PT):
            arrivals[b].wait()
            for s in range(COL_TILES):
                tile = across[:, b, s].reshape(T, T)
                high, low = halves(tile)
                pivot_high[b * T:b * T + T, s * T:s * T + T] = high
                pivot_low[b * T:b * T + T, s * T:s * T + T] = low

        def solve_upper(n, carry):
            part = pl.ds(pl.multiple_of(n * WIDE, WIDE), WIDE)
            for lo, hi in SPLITS:
                high, low = halves(product(
                    (inverse_high[lo:hi, :hi], inverse_low[lo:hi, :hi]),
                    (pivot_high[:hi, part], pivot_low[:hi, part]),
                ))
                upper_high[lo:hi, part] = high
                upper_low[lo:hi, part] = low
            return carry

        lax.fori_loop(0, COL_TILES * T // WIDE, solve_upper, 0)

    mine_halves = halves(lower[...])
    for n in range(COL_TILES * T // WIDE):
        change = product(
            mine_halves,
            (upper_high[:, n * WIDE:n * WIDE + WIDE], upper_low[:, n * WIDE:n * WIDE + WIDE]),
        )
        for s in range(WIDE // T):
            where = pl.ds(n * (WIDE // T) + s, T, stride=COL_TILES)
            out[where, :] = front[where, :] - change[:, s * T:s * T + T]

    @pl.when(t == 0)
    def _():
        for copy in child_copies():
            copy.wait()

    add_children(maps, moved, other, out)
    first = jnp.logical_and(t == 0, row < PT)

    @pl.when(first)
    def _():
        for s in range(COL_TILES):
            out[pl.ds(s, T, stride=COL_TILES), :] = jnp.zeros((T, T), F32)

    @pl.when(j < PT)
    def _():
        tile = lower[:, pl.ds(pl.multiple_of(j * T, T), T)]
        x = lax.broadcasted_iota(jnp.int32, (T, T), 0) + (16 * t + row) * T
        y = lax.broadcasted_iota(jnp.int32, (T, T), 1) + j * T
        out[pl.ds(0, T, stride=COL_TILES), :] = jnp.where(x >= y, tile, 0.0)


def pack_other(maps, orders, moved, child, out, column):
    k, i, j = place()
    order = orders[k]
    for g in range(CHILD_TILES):
        tile = child_tile(child, order, i, j, g, 0)
        column[(8 * g + i + offset(maps, k, g)) % 16] = tile
    rank = jnp.int32(0)
    for g in range(CHILD_TILES):
        shift = offset(maps, k, g)
        source = (i - shift) % 8
        leaves = (8 * g + source + shift) // 8 % 2 != k
        here = jnp.minimum(rank, 3)

        @pl.when(leaves)
        def _():
            for h in range(CHILD_TILES):
                out[here, h] = moved[source * 8 + (j - offset(maps, k, h)) % 8]

        rank = rank + leaves.astype(jnp.int32)


def add_children(maps, moved, other, out):
    k, i, j = place()
    t = pl.program_id(0)

    def add(child, tile_of):
        for h in range(CHILD_TILES):
            across = offset(maps, child, h)
            from_j = (j - across) % 8
            where = pl.ds((8 * h + from_j + across) // 8, T, stride=COL_TILES)
            out[where, :] = out[where, :] + tile_of(h, from_j)

    rank = jnp.int32(0)
    for g in range(CHILD_TILES):
        shift = offset(maps, k, g)
        source = (i - shift) % 8
        p = 8 * g + source + shift
        mine = p // 8 % 2 == k

        @pl.when(jnp.logical_and(mine, p // 16 == t))
        def _():
            add(k, lambda h, from_j: moved[source * 8 + from_j])

        far = 1 - k
        far_shift = offset(maps, far, g)
        far_p = 8 * g + (i - far_shift) % 8 + far_shift
        comes = far_p // 8 % 2 == k
        here = jnp.minimum(rank, 3)

        @pl.when(jnp.logical_and(comes, far_p // 16 == t))
        def _():
            add(far, lambda h, from_j: other[here, h])

        rank = rank + comes.astype(jnp.int32)


def shards(front, child_updates, child_maps, child_orders):
    front = front.reshape(ROW_TILES * T * COL_TILES, T)
    child = child_updates.reshape(CHILD_TILES * T * CHILD_TILES, T)
    maps = child_maps
    main = pl.pallas_call(
        pack_main,
        out_shape=shape(64, T, T),
        in_specs=[SMEM, SMEM, VMEM],
        out_specs=VMEM,
        compiler_params=params(16),
        name="pack_main",
    )(maps, child_orders, child)
    main = lax.all_to_all(main, ("i", "col"), 0, 0, tiled=True)
    other, column = pl.pallas_call(
        pack_other,
        out_shape=(shape(4, CHILD_TILES, T, T), shape(16, T, T)),
        in_specs=[SMEM, SMEM, VMEM, VMEM],
        out_specs=[VMEM, VMEM],
        compiler_params=params(20),
        name="pack_other",
    )(maps, child_orders, main, child)
    column = lax.all_to_all(column, ROWS, 0, 0, tiled=True)
    other = lax.ppermute(other, "k", [(0, 1), (1, 0)])
    panel, column = pl.pallas_call(
        pack_panel,
        out_shape=(shape(16, PIECES, 8, T), shape(ROW_TILES, T, T)),
        in_specs=[SMEM, SMEM, VMEM, VMEM, VMEM],
        out_specs=[VMEM, VMEM],
        compiler_params=params(20),
        name="pack_panel",
    )(maps, child_orders, front, child, column)
    down = lax.all_gather(column, "col")
    panel = lax.all_to_all(panel, ROWS, 0, 0, tiled=True)
    slices = pl.pallas_call(
        pack_slices,
        out_shape=shape(8, 3 * PT, 8, T),
        in_specs=[SMEM, VMEM],
        out_specs=VMEM,
        compiler_params=params(16),
        name="pack_slices",
    )(maps, panel)
    slices = lax.all_to_all(slices, "col", 0, 0, tiled=True)
    slab, lead = pl.pallas_call(
        add_slices,
        out_shape=(shape(PT, COL_TILES, 8, T), shape(16, len(UPPER), 8, T)),
        in_specs=[SMEM, VMEM, VMEM, ANY],
        out_specs=[VMEM, VMEM],
        compiler_params=params(16),
        name="add_slices",
    )(maps, panel, slices, other)
    across = lax.all_gather(slab, ROWS)
    lead = lax.all_to_all(lead, ROWS, 0, 0, tiled=True)
    inverse = pl.pallas_call(
        invert_factor,
        out_shape=shape(PT * T, PT * T),
        in_specs=[VMEM],
        out_specs=VMEM,
        scratch_shapes=[pltpu.VMEM((PT * T, PT * T), F32), pltpu.VMEM((T, 2 * T), F32)],
        compiler_params=params(16),
        cost_estimate=pl.CostEstimate(flops=25 * 10**9, bytes_accessed=4 * 2**20, transcendentals=0),
        name="invert_factor",
    )(lead)
    square = jax.ShapeDtypeStruct((PT * T, PT * T), BF16)
    lower, inverse_high, inverse_low = pl.pallas_call(
        solve_rows,
        out_shape=(shape(ROW_TILES * T, PT * T), square, square),
        in_specs=[VMEM, VMEM],
        out_specs=[VMEM] * 3,
        compiler_params=params(20),
        cost_estimate=pl.CostEstimate(flops=5 * 10**9, bytes_accessed=8 * 2**20, transcendentals=0),
        name="solve_rows",
    )(down, inverse)
    block = pl.BlockSpec((T * COL_TILES, T), lambda t: (t, 0))
    out = pl.pallas_call(
        eliminate,
        out_shape=shape(ROW_TILES * T * COL_TILES, T),
        grid=(ROW_TILES,),
        in_specs=[SMEM, block, ANY, pl.BlockSpec((T, PT * T), lambda t: (t, 0)), VMEM, VMEM, ANY, ANY],
        out_specs=block,
        scratch_shapes=[
            pltpu.VMEM((PT * T, COL_TILES * T), BF16),
            pltpu.VMEM((PT * T, COL_TILES * T), BF16),
            pltpu.VMEM((PT * T, COL_TILES * T), BF16),
            pltpu.VMEM((PT * T, COL_TILES * T), BF16),
            pltpu.VMEM((16, PT, COL_TILES, 8, T), F32),
            pltpu.VMEM((64, T, T), F32),
            pltpu.VMEM((4, CHILD_TILES, T, T), F32),
            pltpu.SemaphoreType.DMA((PT,)),
            pltpu.SemaphoreType.DMA((2,)),
        ],
        compiler_params=params(58),
        cost_estimate=pl.CostEstimate(flops=12 * 10**9, bytes_accessed=20 * 2**20, transcendentals=0),
        name="eliminate",
    )(maps, front, across, lower, inverse_high, inverse_low, main, other)
    return out.reshape(ROW_TILES, 1, T, COL_TILES, 1, T)


def solution(mesh):
    split = Mesh(mesh.devices.reshape(2, 8, 8), ("k", "i", "col"))
    tiles = P(None, ROWS, None, None, "col", None)
    return jax.shard_map(
        shards, mesh=split, in_specs=(tiles, tiles, P(), P()), out_specs=tiles, check_vma=False
    )
```

```python
import jax
import jax.numpy as jnp
from jax import lax
from jax.experimental import pallas as pl
from jax.experimental.pallas import tpu as pltpu
from jax.sharding import Mesh
from jax.sharding import PartitionSpec as P

T = 128
PT = 5
ROW_TILES = 6
COL_TILES = 12
CHILD_TILES = 6
ROWS = ("k", "i")
UPPER = [(b, c) for b in range(PT) for c in range(b, PT)]
GROUP = 32
HIGHEST = lax.Precision.HIGHEST
F32 = jnp.float32
BF16 = jnp.bfloat16

VMEM = pl.BlockSpec(memory_space=pltpu.VMEM)
ANY = pl.BlockSpec(memory_space=pl.ANY)
SMEM = pl.BlockSpec(memory_space=pltpu.SMEM)


def shape(*dims):
    return jax.ShapeDtypeStruct(dims, F32)


def params(mib):
    return pltpu.CompilerParams(vmem_limit_bytes=mib * 2**20)


def place():
    return lax.axis_index("k"), lax.axis_index("i"), lax.axis_index("col")


def offset(maps, child, run):
    return maps[child, 8 * run] - 8 * run


def child_tile(child, order, i, j, g, h):
    tile = child[pl.ds(g * T * CHILD_TILES + h, T, stride=CHILD_TILES), :]
    if g == CHILD_TILES - 1:
        rows = lax.broadcasted_iota(jnp.int32, (T, T), 0) + (8 * g + i) * T
        tile = jnp.where(rows < order, tile, 0.0)
    if h == CHILD_TILES - 1:
        cols = lax.broadcasted_iota(jnp.int32, (T, T), 1) + (8 * h + j) * T
        tile = jnp.where(cols < order, tile, 0.0)
    return tile


def pack_main(maps, orders, child, out):
    k, i, j = place()
    order = orders[k]
    for g in range(CHILD_TILES):
        to_i = (i + offset(maps, k, g)) % 8
        for h in range(CHILD_TILES):
            to_j = (j + offset(maps, k, h)) % 8
            out[to_i * 8 + to_j] = child_tile(child, order, i, j, g, h)


def add_column(maps, front, moved, other, out):
    k, i, j = place()
    for t in range(ROW_TILES):
        out[t] = front[pl.ds(t * T * COL_TILES, T, stride=COL_TILES), :]
    rank = jnp.int32(0)
    for g in range(CHILD_TILES):
        shift = offset(maps, k, g)
        source = (i - shift) % 8
        p = 8 * g + source + shift

        @pl.when(p // 8 % 2 == k)
        def _():
            out[p // 16] = out[p // 16] + moved[source * 8 + j]

        far_shift = offset(maps, 1 - k, g)
        far_p = 8 * g + (i - far_shift) % 8 + far_shift
        comes = far_p // 8 % 2 == k
        here = jnp.minimum(rank, 3)

        @pl.when(comes)
        def _():
            out[far_p // 16] = out[far_p // 16] + other[here]

        rank = rank + comes.astype(jnp.int32)


def pack_rows(maps, front_far, moved_far, other, out, tiles, front, moved, sems):
    k, i, j = place()

    @pl.when(jnp.logical_and(k == 0, i < PT))
    def _():
        copies = (
            pltpu.make_async_copy(front_far.at[pl.ds(0, T * COL_TILES)], front, sems.at[0]),
            pltpu.make_async_copy(moved_far.at[pl.ds(i * 8, 8)], moved, sems.at[1]),
        )
        for copy in copies:
            copy.start()
        for copy in copies:
            copy.wait()
        for s in range(COL_TILES):
            tiles[s] = front[pl.ds(s, T, stride=COL_TILES), :]
        for child in range(2):
            for h in range(CHILD_TILES):
                shift = offset(maps, child, h)
                from_j = (j - shift) % 8
                s = (8 * h + from_j + shift) // 8
                if child == 0:
                    tile = moved[from_j]
                else:
                    tile = other[0 if h == 0 else 3 + h]
                tiles[s] = tiles[s] + tile
        for v in range(16):
            for s in range(COL_TILES):
                out[v, s] = tiles[s, 8 * v:8 * v + 8]


def pack_lead(got, out):
    for n, (b, c) in enumerate(UPPER):
        piece = got[c, b]
        for v in range(16):
            out[v, n] = piece


def reciprocal(x):
    y = pl.reciprocal(x, approx=True)
    y = y * (2.0 - x * y)
    return y * (2.0 - x * y)


def invert_factor(lead, out, matrix, work):
    for n, (b, c) in enumerate(UPPER):
        for r in range(16):
            matrix[b * T + 8 * r:b * T + 8 * r + 8, c * T:c * T + T] = lead[r, n]
    out[...] = jnp.zeros_like(out)
    sub = lax.broadcasted_iota(jnp.int32, (8, T), 0)
    eye = (
        lax.broadcasted_iota(jnp.int32, (T, T), 0) == lax.broadcasted_iota(jnp.int32, (T, T), 1)
    ).astype(F32)
    for b in range(PT):
        lo, hi = b * T, b * T + T
        work[:, :T] = matrix[lo:hi, lo:hi]
        work[:, T:] = eye
        for base in range(0, T, GROUP):
            rows = [work[base + 8 * q:base + 8 * q + 8, :T] for q in range(GROUP // 8)]
            other = [work[base + 8 * q:base + 8 * q + 8, T:] for q in range(GROUP // 8)]
            inverses = []
            for p in range(GROUP // 8):
                first = base + 8 * p
                after = range(p, GROUP // 8)
                columns = {
                    q: [
                        jnp.broadcast_to(rows[q][:, first + m:first + m + 1], (8, T))
                        for m in range(8)
                    ]
                    for q in after
                }
                pivots = jnp.ones((8, T), F32)
                for m in range(8):
                    pivot = jnp.broadcast_to(columns[p][m][m:m + 1, :], (8, T))
                    pivots = jnp.where(sub == m, pivot, pivots)
                    over = reciprocal(pivot)
                    row = jnp.broadcast_to(rows[p][m:m + 1, :], (8, T))
                    mate = jnp.broadcast_to(other[p][m:m + 1, :], (8, T))
                    for n in range(m + 1, 8):
                        head = jnp.broadcast_to(columns[p][n][m:m + 1, :], (8, T))
                        for q in after:
                            scale = columns[q][m] * over
                            if q == p:
                                scale = jnp.where(sub > m, scale, 0.0)
                            columns[q][n] = columns[q][n] - scale * head
                    for q in after:
                        scale = columns[q][m] * over
                        if q == p:
                            if m == 7:
                                continue
                            scale = jnp.where(sub > m, scale, 0.0)
                        rows[q] = rows[q] - scale * row
                        other[q] = other[q] - scale * mate
                out[lo + first:lo + first + 8, lo:hi] = other[p] * lax.rsqrt(pivots)
                inverses.append(1.0 / pivots)
            if base + GROUP < T:
                scaled = jnp.concatenate([x * y for x, y in zip(rows, inverses)], axis=0)
                both = jnp.concatenate(
                    [jnp.concatenate(rows, axis=0), jnp.concatenate(other, axis=0)], axis=1
                )
                change = jnp.dot(
                    scaled.T[base + GROUP:, :], both,
                    precision=HIGHEST, preferred_element_type=F32,
                )
                work[base + GROUP:, :] = work[base + GROUP:, :] - change
        inverse = out[lo:hi, lo:hi]
        if b > 0:
            out[lo:hi, :lo] = jnp.dot(
                inverse, out[lo:hi, :lo], precision=HIGHEST, preferred_element_type=F32
            )
        if b < PT - 1:
            right = jnp.dot(
                inverse, matrix[lo:hi, hi:], precision=HIGHEST, preferred_element_type=F32
            )
            for n in range(b + 1, PT):
                low, high = n * T, n * T + T
                factor = right[:, low - hi:high - hi]
                matrix[low:high, low:] = matrix[low:high, low:] - lax.dot_general(
                    factor, right[:, low - hi:], (((0,), (0,)), ((), ())),
                    precision=HIGHEST, preferred_element_type=F32,
                )
                out[low:high, :hi] = out[low:high, :hi] - lax.dot_general(
                    factor, out[lo:hi, :hi], (((0,), (0,)), ((), ())),
                    precision=HIGHEST, preferred_element_type=F32,
                )


SPLITS = ((0, 256), (256, 512), (512, 640))
WIDE = 512


def halves(x):
    high = x.astype(BF16)
    return high, (x - high.astype(F32)).astype(BF16)


def product(a, b):
    (a_high, a_low), (b_high, b_low) = a, b
    small = jnp.dot(a_high, b_low, preferred_element_type=F32) + jnp.dot(
        a_low, b_high, preferred_element_type=F32
    )
    return jnp.dot(a_high, b_high, preferred_element_type=F32) + small


def solve_rows(down, inverse, lower, inverse_high, inverse_low):
    high, low = halves(inverse[...])
    inverse_high[...] = high
    inverse_low[...] = low

    def solve(t, carry):
        mine = jnp.concatenate([down[b, t] for b in range(PT)], axis=1)
        part = pl.ds(pl.multiple_of(t * T, T), T)
        for lo, hi in SPLITS:
            lower[part, lo:hi] = lax.dot_general(
                mine[:, :hi], inverse[lo:hi, :hi], (((1,), (1,)), ((), ())),
                precision=HIGHEST, preferred_element_type=F32,
            )
        return carry

    lax.fori_loop(0, ROW_TILES, solve, 0)


def eliminate(
    maps, front, across_far, lower, inverse_high, inverse_low,
    moved_far, near, rest, out,
    pivot_high, pivot_low, upper_high, upper_low, across, moved, other, across_sem, sems,
):
    k, i, j = place()
    row = k * 8 + i
    t = pl.program_id(0)

    def child_copies():
        return (
            pltpu.make_async_copy(moved_far, moved, sems.at[0]),
            pltpu.make_async_copy(near.at[pl.ds(0, 4)], other.at[:, 0], sems.at[1]),
            pltpu.make_async_copy(
                near.at[pl.ds(4, CHILD_TILES - 1)], other.at[0, pl.ds(1, CHILD_TILES - 1)], sems.at[2]
            ),
            pltpu.make_async_copy(
                rest, other.at[pl.ds(1, 3), pl.ds(1, CHILD_TILES - 1)], sems.at[3]
            ),
        )

    @pl.when(t == 0)
    def _():
        arrivals = [
            pltpu.make_async_copy(across_far.at[:, b], across.at[:, b], across_sem.at[b])
            for b in range(PT)
        ]
        for copy in (*arrivals, *child_copies()):
            copy.start()
        for b in range(PT):
            arrivals[b].wait()
            for s in range(COL_TILES):
                tile = across[:, b, s].reshape(T, T)
                high, low = halves(tile)
                pivot_high[b * T:b * T + T, s * T:s * T + T] = high
                pivot_low[b * T:b * T + T, s * T:s * T + T] = low

        def solve_upper(n, carry):
            part = pl.ds(pl.multiple_of(n * WIDE, WIDE), WIDE)
            for lo, hi in SPLITS:
                high, low = halves(product(
                    (inverse_high[lo:hi, :hi], inverse_low[lo:hi, :hi]),
                    (pivot_high[:hi, part], pivot_low[:hi, part]),
                ))
                upper_high[lo:hi, part] = high
                upper_low[lo:hi, part] = low
            return carry

        lax.fori_loop(0, COL_TILES * T // WIDE, solve_upper, 0)

    mine_halves = halves(lower[...])
    for n in range(COL_TILES * T // WIDE):
        change = product(
            mine_halves,
            (upper_high[:, n * WIDE:n * WIDE + WIDE], upper_low[:, n * WIDE:n * WIDE + WIDE]),
        )
        for s in range(WIDE // T):
            where = pl.ds(n * (WIDE // T) + s, T, stride=COL_TILES)
            out[where, :] = front[where, :] - change[:, s * T:s * T + T]

    @pl.when(t == 0)
    def _():
        for copy in child_copies():
            copy.wait()

    add_children(maps, moved, other, out)

    @pl.when(jnp.logical_and(t == 0, row < PT))
    def _():
        for s in range(COL_TILES):
            out[pl.ds(s, T, stride=COL_TILES), :] = jnp.zeros((T, T), F32)

    @pl.when(j < PT)
    def _():
        tile = lower[:, pl.ds(pl.multiple_of(j * T, T), T)]
        x = lax.broadcasted_iota(jnp.int32, (T, T), 0) + (16 * t + row) * T
        y = lax.broadcasted_iota(jnp.int32, (T, T), 1) + j * T
        out[pl.ds(0, T, stride=COL_TILES), :] = jnp.where(x >= y, tile, 0.0)


def pack_other(maps, moved, near, rest):
    k, i, j = place()
    rank = jnp.int32(0)
    for g in range(CHILD_TILES):
        shift = offset(maps, k, g)
        source = (i - shift) % 8
        leaves = (8 * g + source + shift) // 8 % 2 != k
        here = jnp.minimum(rank, 3)

        @pl.when(leaves)
        def _():
            near[here] = moved[source * 8 + j]

        @pl.when(jnp.logical_and(leaves, rank == 0))
        def _():
            for h in range(1, CHILD_TILES):
                near[3 + h] = moved[source * 8 + (j - offset(maps, k, h)) % 8]

        @pl.when(jnp.logical_and(leaves, rank > 0))
        def _():
            for h in range(1, CHILD_TILES):
                rest[jnp.maximum(here - 1, 0), h - 1] = moved[
                    source * 8 + (j - offset(maps, k, h)) % 8
                ]

        rank = rank + leaves.astype(jnp.int32)


def add_children(maps, moved, other, out):
    k, i, j = place()
    t = pl.program_id(0)

    def add(child, tile_of):
        for h in range(CHILD_TILES):
            across = offset(maps, child, h)
            from_j = (j - across) % 8
            where = pl.ds((8 * h + from_j + across) // 8, T, stride=COL_TILES)
            out[where, :] = out[where, :] + tile_of(h, from_j)

    rank = jnp.int32(0)
    for g in range(CHILD_TILES):
        shift = offset(maps, k, g)
        source = (i - shift) % 8
        p = 8 * g + source + shift
        mine = p // 8 % 2 == k

        @pl.when(jnp.logical_and(mine, p // 16 == t))
        def _():
            add(k, lambda h, from_j: moved[source * 8 + from_j])

        far = 1 - k
        far_shift = offset(maps, far, g)
        far_p = 8 * g + (i - far_shift) % 8 + far_shift
        comes = far_p // 8 % 2 == k
        here = jnp.minimum(rank, 3)

        @pl.when(jnp.logical_and(comes, far_p // 16 == t))
        def _():
            add(far, lambda h, from_j: other[here, h])

        rank = rank + comes.astype(jnp.int32)


def shards(front, child_updates, child_maps, child_orders):
    front = front.reshape(ROW_TILES * T * COL_TILES, T)
    child = child_updates.reshape(CHILD_TILES * T * CHILD_TILES, T)
    maps = child_maps
    main = pl.pallas_call(
        pack_main,
        out_shape=shape(64, T, T),
        in_specs=[SMEM, SMEM, VMEM],
        out_specs=VMEM,
        compiler_params=params(16),
        name="pack_main",
    )(maps, child_orders, child)
    main = lax.all_to_all(main, ("i", "col"), 0, 0, tiled=True)
    swap = [(0, 1), (1, 0)]
    near, rest = pl.pallas_call(
        pack_other,
        out_shape=(shape(3 + CHILD_TILES, T, T), shape(3, CHILD_TILES - 1, T, T)),
        in_specs=[SMEM, VMEM],
        out_specs=[VMEM] * 2,
        compiler_params=params(16),
        name="pack_other",
    )(maps, main)
    near = lax.ppermute(near, "k", swap)
    rest = lax.ppermute(rest, "k", swap)
    column = pl.pallas_call(
        add_column,
        out_shape=shape(ROW_TILES, T, T),
        in_specs=[SMEM, VMEM, VMEM, VMEM],
        out_specs=VMEM,
        compiler_params=params(16),
        name="add_column",
    )(maps, front, main, near)
    down = lax.all_gather(column, "col")
    rows = pl.pallas_call(
        pack_rows,
        out_shape=shape(16, COL_TILES, 8, T),
        in_specs=[SMEM, ANY, ANY, VMEM],
        out_specs=VMEM,
        scratch_shapes=[
            pltpu.VMEM((COL_TILES, T, T), F32),
            pltpu.VMEM((T * COL_TILES, T), F32),
            pltpu.VMEM((8, T, T), F32),
            pltpu.SemaphoreType.DMA((2,)),
        ],
        compiler_params=params(58),
        name="pack_rows",
    )(maps, front, main, near)
    rows = lax.all_to_all(rows, ROWS, 0, 0, tiled=True)
    slab = rows[:PT]
    across = lax.all_gather(slab, ROWS)
    lead = lax.all_gather(slab[:, 0], "col")
    lead = pl.pallas_call(
        pack_lead,
        out_shape=shape(16, len(UPPER), 8, T),
        in_specs=[VMEM],
        out_specs=VMEM,
        compiler_params=params(16),
        name="pack_lead",
    )(lead)
    lead = lax.all_to_all(lead, ROWS, 0, 0, tiled=True)
    inverse = pl.pallas_call(
        invert_factor,
        out_shape=shape(PT * T, PT * T),
        in_specs=[VMEM],
        out_specs=VMEM,
        scratch_shapes=[pltpu.VMEM((PT * T, PT * T), F32), pltpu.VMEM((T, 2 * T), F32)],
        compiler_params=params(16),
        cost_estimate=pl.CostEstimate(flops=25 * 10**9, bytes_accessed=4 * 2**20, transcendentals=0),
        name="invert_factor",
    )(lead)
    square = jax.ShapeDtypeStruct((PT * T, PT * T), BF16)
    lower, inverse_high, inverse_low = pl.pallas_call(
        solve_rows,
        out_shape=(shape(ROW_TILES * T, PT * T), square, square),
        in_specs=[VMEM, VMEM],
        out_specs=[VMEM] * 3,
        compiler_params=params(20),
        cost_estimate=pl.CostEstimate(flops=5 * 10**9, bytes_accessed=8 * 2**20, transcendentals=0),
        name="solve_rows",
    )(down, inverse)
    block = pl.BlockSpec((T * COL_TILES, T), lambda t: (t, 0))
    out = pl.pallas_call(
        eliminate,
        out_shape=shape(ROW_TILES * T * COL_TILES, T),
        grid=(ROW_TILES,),
        in_specs=[SMEM, block, ANY, pl.BlockSpec((T, PT * T), lambda t: (t, 0))] + [VMEM] * 2 + [ANY] * 3,
        out_specs=block,
        scratch_shapes=[
            pltpu.VMEM((PT * T, COL_TILES * T), BF16),
            pltpu.VMEM((PT * T, COL_TILES * T), BF16),
            pltpu.VMEM((PT * T, COL_TILES * T), BF16),
            pltpu.VMEM((PT * T, COL_TILES * T), BF16),
            pltpu.VMEM((16, PT, COL_TILES, 8, T), F32),
            pltpu.VMEM((64, T, T), F32),
            pltpu.VMEM((4, CHILD_TILES, T, T), F32),
            pltpu.SemaphoreType.DMA((PT,)),
            pltpu.SemaphoreType.DMA((4,)),
        ],
        compiler_params=params(58),
        cost_estimate=pl.CostEstimate(flops=12 * 10**9, bytes_accessed=20 * 2**20, transcendentals=0),
        name="eliminate",
    )(maps, front, across, lower, inverse_high, inverse_low, main, near, rest)
    return out.reshape(ROW_TILES, 1, T, COL_TILES, 1, T)


def solution(mesh):
    split = Mesh(mesh.devices.reshape(2, 8, 8), ("k", "i", "col"))
    tiles = P(None, ROWS, None, None, "col", None)
    return jax.shard_map(
        shards, mesh=split, in_specs=(tiles, tiles, P(), P()), out_specs=tiles, check_vma=False
    )
```

```python
import jax
import jax.numpy as jnp
from jax import lax
from jax.experimental import pallas as pl
from jax.experimental.pallas import tpu as pltpu
from jax.sharding import Mesh
from jax.sharding import PartitionSpec as P

T = 128
PT = 5
ROW_TILES = 6
COL_TILES = 12
CHILD_TILES = 6
ROWS = ("k", "i")
UPPER = [(b, c) for b in range(PT) for c in range(b, PT)]
GROUP = 32
HIGHEST = lax.Precision.HIGHEST
F32 = jnp.float32
BF16 = jnp.bfloat16

VMEM = pl.BlockSpec(memory_space=pltpu.VMEM)
ANY = pl.BlockSpec(memory_space=pl.ANY)
SMEM = pl.BlockSpec(memory_space=pltpu.SMEM)


def shape(*dims):
    return jax.ShapeDtypeStruct(dims, F32)


def params(mib):
    return pltpu.CompilerParams(vmem_limit_bytes=mib * 2**20)


def place():
    return lax.axis_index("k"), lax.axis_index("i"), lax.axis_index("col")


def offset(maps, child, run):
    return maps[child, 8 * run] - 8 * run


def child_tile(child, order, i, j, g, h):
    tile = child[pl.ds(g * T * CHILD_TILES + h, T, stride=CHILD_TILES), :]
    if g == CHILD_TILES - 1:
        rows = lax.broadcasted_iota(jnp.int32, (T, T), 0) + (8 * g + i) * T
        tile = jnp.where(rows < order, tile, 0.0)
    if h == CHILD_TILES - 1:
        cols = lax.broadcasted_iota(jnp.int32, (T, T), 1) + (8 * h + j) * T
        tile = jnp.where(cols < order, tile, 0.0)
    return tile


def pack_main(maps, orders, child, out):
    k, i, j = place()
    order = orders[k]
    for g in range(CHILD_TILES):
        to_i = (i + offset(maps, k, g)) % 8
        for h in range(CHILD_TILES):
            to_j = (j + offset(maps, k, h)) % 8
            out[to_i * 8 + to_j] = child_tile(child, order, i, j, g, h)


def add_column(maps, front, moved, other, lead, out):
    k, i, j = place()

    def tile(t):
        return pl.ds(pl.multiple_of(t * T, T), T)

    for b in range(PT):
        first = ROW_TILES * T + 8 * b
        out[first:first + 8, :] = lead[b] + lead[8 + b]
    for t in range(ROW_TILES):
        out[t * T:t * T + T, :] = front[pl.ds(t * T * COL_TILES, T, stride=COL_TILES), :]
    rank = jnp.int32(0)
    for g in range(CHILD_TILES):
        shift = offset(maps, k, g)
        source = (i - shift) % 8
        p = 8 * g + source + shift

        @pl.when(p // 8 % 2 == k)
        def _():
            out[tile(p // 16), :] = out[tile(p // 16), :] + moved[source * 8 + j]

        far_shift = offset(maps, 1 - k, g)
        far_p = 8 * g + (i - far_shift) % 8 + far_shift
        comes = far_p // 8 % 2 == k
        here = jnp.minimum(rank, 3)

        @pl.when(comes)
        def _():
            out[tile(far_p // 16), :] = out[tile(far_p // 16), :] + other[here]

        rank = rank + comes.astype(jnp.int32)


def pack_rows(maps, front_far, moved_far, other, out, tiles, front, moved, sems):
    k, i, j = place()

    @pl.when(jnp.logical_and(k == 0, i < PT))
    def _():
        copies = (
            pltpu.make_async_copy(front_far.at[pl.ds(0, T * COL_TILES)], front, sems.at[0]),
            pltpu.make_async_copy(moved_far.at[pl.ds(i * 8, 8)], moved, sems.at[1]),
        )
        for copy in copies:
            copy.start()
        for copy in copies:
            copy.wait()
        for s in range(COL_TILES):
            tiles[s] = front[pl.ds(s, T, stride=COL_TILES), :]
        for child in range(2):
            for h in range(CHILD_TILES):
                shift = offset(maps, child, h)
                from_j = (j - shift) % 8
                s = (8 * h + from_j + shift) // 8
                if child == 0:
                    tile = moved[from_j]
                else:
                    tile = other[0 if h == 0 else 3 + h]
                tiles[s] = tiles[s] + tile
        for v in range(16):
            for s in range(COL_TILES):
                out[v, s] = tiles[s, 8 * v:8 * v + 8]


def take_slab(rows, other, out):
    for b in range(PT):
        out[b] = rows[b]


def pack_lead(far, out, got, sem):
    copy = pltpu.make_async_copy(
        far.at[pl.ds(0, PT), pl.ds(ROW_TILES * T, 8 * PT)], got, sem
    )
    copy.start()
    copy.wait()
    for n, (b, c) in enumerate(UPPER):
        piece = got[c, 8 * b:8 * b + 8]
        for v in range(16):
            out[v, n] = piece


SPLITS = ((0, 256), (256, 512), (512, 640))
WIDE = 512


def halves(x):
    high = x.astype(BF16)
    return high, (x - high.astype(F32)).astype(BF16)


def product(a, b, over=0):
    (a_high, a_low), (b_high, b_low) = a, b

    def dot(x, y):
        return lax.dot_general(x, y, (((1,), (over,)), ((), ())), preferred_element_type=F32)

    return dot(a_high, b_high) + (dot(a_high, b_low) + dot(a_low, b_high))


def reciprocal(x):
    y = pl.reciprocal(x, approx=True)
    y = y * (2.0 - x * y)
    return y * (2.0 - x * y)


def invert_factor(lead, far, lower, inverse_high, inverse_low, out, matrix, work, down, sem):
    copy = pltpu.make_async_copy(far.at[pl.ds(0, PT), pl.ds(0, ROW_TILES * T)], down, sem)
    copy.start()
    for n, (b, c) in enumerate(UPPER):
        for r in range(16):
            matrix[b * T + 8 * r:b * T + 8 * r + 8, c * T:c * T + T] = lead[r, n]
    out[...] = jnp.zeros_like(out)
    sub = lax.broadcasted_iota(jnp.int32, (8, T), 0)
    eye = (
        lax.broadcasted_iota(jnp.int32, (T, T), 0) == lax.broadcasted_iota(jnp.int32, (T, T), 1)
    ).astype(F32)
    for b in range(PT):
        lo, hi = b * T, b * T + T
        work[:, :T] = matrix[lo:hi, lo:hi]
        work[:, T:] = eye
        for base in range(0, T, GROUP):
            rows = [work[base + 8 * q:base + 8 * q + 8, :T] for q in range(GROUP // 8)]
            other = [work[base + 8 * q:base + 8 * q + 8, T:] for q in range(GROUP // 8)]
            inverses = []
            for p in range(GROUP // 8):
                first = base + 8 * p
                after = range(p, GROUP // 8)
                columns = {
                    q: [
                        jnp.broadcast_to(rows[q][:, first + m:first + m + 1], (8, T))
                        for m in range(8)
                    ]
                    for q in after
                }
                pivots = jnp.ones((8, T), F32)
                for m in range(8):
                    pivot = jnp.broadcast_to(columns[p][m][m:m + 1, :], (8, T))
                    pivots = jnp.where(sub == m, pivot, pivots)
                    over = reciprocal(pivot)
                    row = jnp.broadcast_to(rows[p][m:m + 1, :], (8, T))
                    mate = jnp.broadcast_to(other[p][m:m + 1, :], (8, T))
                    for n in range(m + 1, 8):
                        head = jnp.broadcast_to(columns[p][n][m:m + 1, :], (8, T))
                        for q in after:
                            scale = columns[q][m] * over
                            if q == p:
                                scale = jnp.where(sub > m, scale, 0.0)
                            columns[q][n] = columns[q][n] - scale * head
                    for q in after:
                        scale = columns[q][m] * over
                        if q == p:
                            if m == 7:
                                continue
                            scale = jnp.where(sub > m, scale, 0.0)
                        rows[q] = rows[q] - scale * row
                        other[q] = other[q] - scale * mate
                out[lo + first:lo + first + 8, lo:hi] = other[p] * lax.rsqrt(pivots)
                inverses.append(1.0 / pivots)
            if base + GROUP < T:
                scaled = jnp.concatenate([x * y for x, y in zip(rows, inverses)], axis=0)
                both = jnp.concatenate(
                    [jnp.concatenate(rows, axis=0), jnp.concatenate(other, axis=0)], axis=1
                )
                change = jnp.dot(
                    scaled.T[base + GROUP:, :], both,
                    precision=HIGHEST, preferred_element_type=F32,
                )
                work[base + GROUP:, :] = work[base + GROUP:, :] - change
        inverse = out[lo:hi, lo:hi]
        if b > 0:
            out[lo:hi, :lo] = jnp.dot(
                inverse, out[lo:hi, :lo], precision=HIGHEST, preferred_element_type=F32
            )
        if b < PT - 1:
            right = jnp.dot(
                inverse, matrix[lo:hi, hi:], precision=HIGHEST, preferred_element_type=F32
            )
            for n in range(b + 1, PT):
                low, high = n * T, n * T + T
                factor = right[:, low - hi:high - hi]
                matrix[low:high, low:] = matrix[low:high, low:] - lax.dot_general(
                    factor, right[:, low - hi:], (((0,), (0,)), ((), ())),
                    precision=HIGHEST, preferred_element_type=F32,
                )
                out[low:high, :hi] = out[low:high, :hi] - lax.dot_general(
                    factor, out[lo:hi, :hi], (((0,), (0,)), ((), ())),
                    precision=HIGHEST, preferred_element_type=F32,
                )


    high, low = halves(out[...])
    inverse_high[...] = high
    inverse_low[...] = low
    copy.wait()

    def solve(t, carry):
        part = pl.ds(pl.multiple_of(t * T, T), T)
        mine_high, mine_low = halves(jnp.concatenate([down[b, part, :] for b in range(PT)], axis=1))
        for lo, hi in SPLITS:
            lower[part, lo:hi] = product(
                (mine_high[:, :hi], mine_low[:, :hi]),
                (inverse_high[lo:hi, :hi], inverse_low[lo:hi, :hi]),
                1,
            )
        return carry

    lax.fori_loop(0, ROW_TILES, solve, 0)


def eliminate(
    maps, front, across_far, lower, inverse_high, inverse_low,
    moved_far, near, rest, out,
    pivot_high, pivot_low, upper_high, upper_low, across, moved, other, across_sem, sems,
):
    k, i, j = place()
    row = k * 8 + i
    t = pl.program_id(0)

    def child_copies():
        return (
            pltpu.make_async_copy(moved_far, moved, sems.at[0]),
            pltpu.make_async_copy(near.at[pl.ds(0, 4)], other.at[:, 0], sems.at[1]),
            pltpu.make_async_copy(
                near.at[pl.ds(4, CHILD_TILES - 1)], other.at[0, pl.ds(1, CHILD_TILES - 1)], sems.at[2]
            ),
            pltpu.make_async_copy(
                rest, other.at[pl.ds(1, 3), pl.ds(1, CHILD_TILES - 1)], sems.at[3]
            ),
        )

    @pl.when(t == 0)
    def _():
        arrivals = [
            pltpu.make_async_copy(across_far.at[:, b], across.at[:, b], across_sem.at[b])
            for b in range(PT)
        ]
        for copy in (*arrivals, *child_copies()):
            copy.start()
        for b in range(PT):
            arrivals[b].wait()
            for s in range(COL_TILES):
                tile = across[:, b, s].reshape(T, T)
                high, low = halves(tile)
                pivot_high[b * T:b * T + T, s * T:s * T + T] = high
                pivot_low[b * T:b * T + T, s * T:s * T + T] = low

        def solve_upper(n, carry):
            part = pl.ds(pl.multiple_of(n * WIDE, WIDE), WIDE)
            for lo, hi in SPLITS:
                high, low = halves(product(
                    (inverse_high[lo:hi, :hi], inverse_low[lo:hi, :hi]),
                    (pivot_high[:hi, part], pivot_low[:hi, part]),
                ))
                upper_high[lo:hi, part] = high
                upper_low[lo:hi, part] = low
            return carry

        lax.fori_loop(0, COL_TILES * T // WIDE, solve_upper, 0)

    mine_halves = halves(lower[...])
    for n in range(COL_TILES * T // WIDE):
        change = product(
            mine_halves,
            (upper_high[:, n * WIDE:n * WIDE + WIDE], upper_low[:, n * WIDE:n * WIDE + WIDE]),
        )
        for s in range(WIDE // T):
            where = pl.ds(n * (WIDE // T) + s, T, stride=COL_TILES)
            out[where, :] = front[where, :] - change[:, s * T:s * T + T]

    @pl.when(t == 0)
    def _():
        for copy in child_copies():
            copy.wait()

    add_children(maps, moved, other, out)

    @pl.when(jnp.logical_and(t == 0, row < PT))
    def _():
        for s in range(COL_TILES):
            out[pl.ds(s, T, stride=COL_TILES), :] = jnp.zeros((T, T), F32)

    @pl.when(j < PT)
    def _():
        tile = lower[:, pl.ds(pl.multiple_of(j * T, T), T)]
        x = lax.broadcasted_iota(jnp.int32, (T, T), 0) + (16 * t + row) * T
        y = lax.broadcasted_iota(jnp.int32, (T, T), 1) + j * T
        out[pl.ds(0, T, stride=COL_TILES), :] = jnp.where(x >= y, tile, 0.0)


def pack_other(maps, moved, child, front, near, rest, lead):
    k, i, j = place()
    tile = child[pl.ds(0, T, stride=CHILD_TILES), :]
    tile = tile + jnp.where(k == 0, front[pl.ds(0, T, stride=COL_TILES), :], 0.0)
    for v in range(16):
        lead[v] = tile[8 * v:8 * v + 8]
    rank = jnp.int32(0)
    for g in range(CHILD_TILES):
        shift = offset(maps, k, g)
        source = (i - shift) % 8
        leaves = (8 * g + source + shift) // 8 % 2 != k
        here = jnp.minimum(rank, 3)

        @pl.when(leaves)
        def _():
            near[here] = moved[source * 8 + j]

        @pl.when(jnp.logical_and(leaves, rank == 0))
        def _():
            for h in range(1, CHILD_TILES):
                near[3 + h] = moved[source * 8 + (j - offset(maps, k, h)) % 8]

        @pl.when(jnp.logical_and(leaves, rank > 0))
        def _():
            for h in range(1, CHILD_TILES):
                rest[jnp.maximum(here - 1, 0), h - 1] = moved[
                    source * 8 + (j - offset(maps, k, h)) % 8
                ]

        rank = rank + leaves.astype(jnp.int32)


def add_children(maps, moved, other, out):
    k, i, j = place()
    t = pl.program_id(0)

    def add(child, tile_of):
        for h in range(CHILD_TILES):
            across = offset(maps, child, h)
            from_j = (j - across) % 8
            where = pl.ds((8 * h + from_j + across) // 8, T, stride=COL_TILES)
            out[where, :] = out[where, :] + tile_of(h, from_j)

    rank = jnp.int32(0)
    for g in range(CHILD_TILES):
        shift = offset(maps, k, g)
        source = (i - shift) % 8
        p = 8 * g + source + shift
        mine = p // 8 % 2 == k

        @pl.when(jnp.logical_and(mine, p // 16 == t))
        def _():
            add(k, lambda h, from_j: moved[source * 8 + from_j])

        far = 1 - k
        far_shift = offset(maps, far, g)
        far_p = 8 * g + (i - far_shift) % 8 + far_shift
        comes = far_p // 8 % 2 == k
        here = jnp.minimum(rank, 3)

        @pl.when(jnp.logical_and(comes, far_p // 16 == t))
        def _():
            add(far, lambda h, from_j: other[here, h])

        rank = rank + comes.astype(jnp.int32)


def shards(front, child_updates, child_maps, child_orders):
    front = front.reshape(ROW_TILES * T * COL_TILES, T)
    child = child_updates.reshape(CHILD_TILES * T * CHILD_TILES, T)
    maps = child_maps
    main = pl.pallas_call(
        pack_main,
        out_shape=shape(64, T, T),
        in_specs=[SMEM, SMEM, VMEM],
        out_specs=VMEM,
        compiler_params=params(16),
        name="pack_main",
    )(maps, child_orders, child)
    main = lax.all_to_all(main, ("i", "col"), 0, 0, tiled=True)
    swap = [(0, 1), (1, 0)]
    near, rest, lead = pl.pallas_call(
        pack_other,
        out_shape=(
            shape(3 + CHILD_TILES, T, T), shape(3, CHILD_TILES - 1, T, T), shape(16, 8, T)
        ),
        in_specs=[SMEM, VMEM, VMEM, VMEM],
        out_specs=[VMEM] * 3,
        compiler_params=params(16),
        name="pack_other",
    )(maps, main, child, front)
    lead = lax.all_to_all(lead, ROWS, 0, 0, tiled=True)
    near = lax.ppermute(near, "k", swap)
    rest = lax.ppermute(rest, "k", swap)
    column = pl.pallas_call(
        add_column,
        out_shape=shape(ROW_TILES * T + 8 * PT, T),
        in_specs=[SMEM, VMEM, VMEM, VMEM, VMEM],
        out_specs=VMEM,
        compiler_params=params(16),
        name="add_column",
    )(maps, front, main, near, lead)
    down = lax.all_gather(column, "col")
    rows = pl.pallas_call(
        pack_rows,
        out_shape=shape(16, COL_TILES, 8, T),
        in_specs=[SMEM, ANY, ANY, VMEM],
        out_specs=VMEM,
        scratch_shapes=[
            pltpu.VMEM((COL_TILES, T, T), F32),
            pltpu.VMEM((T * COL_TILES, T), F32),
            pltpu.VMEM((8, T, T), F32),
            pltpu.SemaphoreType.DMA((2,)),
        ],
        compiler_params=params(58),
        name="pack_rows",
    )(maps, front, main, near)
    rows = lax.all_to_all(rows, ROWS, 0, 0, tiled=True)
    slab = pl.pallas_call(
        take_slab,
        out_shape=shape(PT, COL_TILES, 8, T),
        in_specs=[VMEM, ANY],
        out_specs=VMEM,
        compiler_params=params(16),
        name="take_slab",
    )(rows, rest)
    across = lax.all_gather(slab, ROWS)
    lead = pl.pallas_call(
        pack_lead,
        out_shape=shape(16, len(UPPER), 8, T),
        in_specs=[ANY],
        out_specs=VMEM,
        scratch_shapes=[pltpu.VMEM((PT, 8 * PT, T), F32), pltpu.SemaphoreType.DMA],
        compiler_params=params(58),
        name="pack_lead",
    )(down)
    lead = lax.all_to_all(lead, ROWS, 0, 0, tiled=True)
    square = jax.ShapeDtypeStruct((PT * T, PT * T), BF16)
    lower, inverse_high, inverse_low = pl.pallas_call(
        invert_factor,
        out_shape=(shape(ROW_TILES * T, PT * T), square, square),
        in_specs=[VMEM, ANY],
        out_specs=[VMEM] * 3,
        scratch_shapes=[
            pltpu.VMEM((PT * T, PT * T), F32),
            pltpu.VMEM((PT * T, PT * T), F32),
            pltpu.VMEM((T, 2 * T), F32),
            pltpu.VMEM((PT, ROW_TILES * T, T), F32),
            pltpu.SemaphoreType.DMA,
        ],
        compiler_params=params(58),
        cost_estimate=pl.CostEstimate(flops=30 * 10**9, bytes_accessed=8 * 2**20, transcendentals=0),
        name="invert_factor",
    )(lead, down)
    block = pl.BlockSpec((T * COL_TILES, T), lambda t: (t, 0))
    out = pl.pallas_call(
        eliminate,
        out_shape=shape(ROW_TILES * T * COL_TILES, T),
        grid=(ROW_TILES,),
        in_specs=[SMEM, block, ANY, pl.BlockSpec((T, PT * T), lambda t: (t, 0))] + [VMEM] * 2 + [ANY] * 3,
        out_specs=block,
        scratch_shapes=[
            pltpu.VMEM((PT * T, COL_TILES * T), BF16),
            pltpu.VMEM((PT * T, COL_TILES * T), BF16),
            pltpu.VMEM((PT * T, COL_TILES * T), BF16),
            pltpu.VMEM((PT * T, COL_TILES * T), BF16),
            pltpu.VMEM((16, PT, COL_TILES, 8, T), F32),
            pltpu.VMEM((64, T, T), F32),
            pltpu.VMEM((4, CHILD_TILES, T, T), F32),
            pltpu.SemaphoreType.DMA((PT,)),
            pltpu.SemaphoreType.DMA((4,)),
        ],
        compiler_params=params(58),
        cost_estimate=pl.CostEstimate(flops=12 * 10**9, bytes_accessed=20 * 2**20, transcendentals=0),
        name="eliminate",
    )(maps, front, across, lower, inverse_high, inverse_low, main, near, rest)
    return out.reshape(ROW_TILES, 1, T, COL_TILES, 1, T)


def solution(mesh):
    split = Mesh(mesh.devices.reshape(2, 8, 8), ("k", "i", "col"))
    tiles = P(None, ROWS, None, None, "col", None)
    return jax.shard_map(
        shards, mesh=split, in_specs=(tiles, tiles, P(), P()), out_specs=tiles, check_vma=False
    )
```

```python
import jax
import jax.numpy as jnp
from jax import lax
from jax.experimental import pallas as pl
from jax.experimental.pallas import tpu as pltpu
from jax.sharding import Mesh
from jax.sharding import PartitionSpec as P

T = 128
PT = 5
ROW_TILES = 6
COL_TILES = 12
CHILD_TILES = 6
ROWS = ("k", "i")
UPPER = [(b, c) for b in range(PT) for c in range(b, PT)]
GROUP = 32
BLOCK = 2
HIGHEST = lax.Precision.HIGHEST
F32 = jnp.float32
BF16 = jnp.bfloat16

VMEM = pl.BlockSpec(memory_space=pltpu.VMEM)
ANY = pl.BlockSpec(memory_space=pl.ANY)
SMEM = pl.BlockSpec(memory_space=pltpu.SMEM)


def shape(*dims):
    return jax.ShapeDtypeStruct(dims, F32)


def params(mib):
    return pltpu.CompilerParams(vmem_limit_bytes=mib * 2**20)


def place():
    return lax.axis_index("k"), lax.axis_index("i"), lax.axis_index("col")


def offset(maps, child, run):
    return maps[child, 8 * run] - 8 * run


def child_tile(child, order, i, j, g, h):
    tile = child[pl.ds(g * T * CHILD_TILES + h, T, stride=CHILD_TILES), :]
    if g == CHILD_TILES - 1:
        rows = lax.broadcasted_iota(jnp.int32, (T, T), 0) + (8 * g + i) * T
        tile = jnp.where(rows < order, tile, 0.0)
    if h == CHILD_TILES - 1:
        cols = lax.broadcasted_iota(jnp.int32, (T, T), 1) + (8 * h + j) * T
        tile = jnp.where(cols < order, tile, 0.0)
    return tile


def pack_main(maps, orders, child, out):
    k, i, j = place()
    order = orders[k]
    for g in range(CHILD_TILES):
        to_i = (i + offset(maps, k, g)) % 8
        for h in range(CHILD_TILES):
            to_j = (j + offset(maps, k, h)) % 8
            out[to_i * 8 + to_j] = child_tile(child, order, i, j, g, h)


def add_column(maps, front, moved, other, lead, out):
    k, i, j = place()

    def tile(t):
        return pl.ds(pl.multiple_of(t * T, T), T)

    for b in range(PT):
        first = ROW_TILES * T + 8 * b
        out[first:first + 8, :] = lead[b] + lead[8 + b]
    for t in range(ROW_TILES):
        out[t * T:t * T + T, :] = front[pl.ds(t * T * COL_TILES, T, stride=COL_TILES), :]
    rank = jnp.int32(0)
    for g in range(CHILD_TILES):
        shift = offset(maps, k, g)
        source = (i - shift) % 8
        p = 8 * g + source + shift

        @pl.when(p // 8 % 2 == k)
        def _():
            out[tile(p // 16), :] = out[tile(p // 16), :] + moved[source * 8 + j]

        far_shift = offset(maps, 1 - k, g)
        far_p = 8 * g + (i - far_shift) % 8 + far_shift
        comes = far_p // 8 % 2 == k
        here = jnp.minimum(rank, 3)

        @pl.when(comes)
        def _():
            out[tile(far_p // 16), :] = out[tile(far_p // 16), :] + other[here]

        rank = rank + comes.astype(jnp.int32)


def pack_rows(maps, front_far, moved_far, other, out, tiles, front, moved, sems):
    k, i, j = place()

    @pl.when(jnp.logical_and(k == 0, i < PT))
    def _():
        copies = (
            pltpu.make_async_copy(front_far.at[pl.ds(0, T * COL_TILES)], front, sems.at[0]),
            pltpu.make_async_copy(moved_far.at[pl.ds(i * 8, 8)], moved, sems.at[1]),
        )
        for copy in copies:
            copy.start()
        for copy in copies:
            copy.wait()
        for s in range(COL_TILES):
            tiles[s] = front[pl.ds(s, T, stride=COL_TILES), :]
        for child in range(2):
            for h in range(CHILD_TILES):
                shift = offset(maps, child, h)
                from_j = (j - shift) % 8
                s = (8 * h + from_j + shift) // 8
                if child == 0:
                    tile = moved[from_j]
                else:
                    tile = other[0 if h == 0 else 3 + h]
                tiles[s] = tiles[s] + tile
        for v in range(16):
            for s in range(COL_TILES):
                out[v, s] = tiles[s, 8 * v:8 * v + 8]


def take_slab(rows, other, out):
    for b in range(PT):
        out[b] = rows[b]


def pack_lead(far, out, got, sem):
    copy = pltpu.make_async_copy(
        far.at[pl.ds(0, PT), pl.ds(ROW_TILES * T, 8 * PT)], got, sem
    )
    copy.start()
    copy.wait()
    for n, (b, c) in enumerate(UPPER):
        piece = got[c, 8 * b:8 * b + 8]
        for v in range(16):
            out[v, n] = piece


SPLITS = ((0, 256), (256, 512), (512, 640))
WIDE = 512


def halves(x):
    high = x.astype(BF16)
    return high, (x - high.astype(F32)).astype(BF16)


def product(a, b, over=0):
    (a_high, a_low), (b_high, b_low) = a, b

    def dot(x, y):
        return lax.dot_general(x, y, (((1,), (over,)), ((), ())), preferred_element_type=F32)

    return dot(a_high, b_high) + (dot(a_high, b_low) + dot(a_low, b_high))


def reciprocal(x):
    y = pl.reciprocal(x, approx=True)
    y = y * (2.0 - x * y)
    return y * (2.0 - x * y)


def split_rows(far, down_high, down_low, down, sems):
    copies = [
        pltpu.make_async_copy(far.at[b, pl.ds(0, ROW_TILES * T)], down.at[b], sems.at[b])
        for b in range(PT)
    ]
    for copy in copies:
        copy.start()
    for b in range(PT):
        copies[b].wait()
        high, low = halves(down[b])
        down_high[:, b * T:b * T + T] = high
        down_low[:, b * T:b * T + T] = low


def invert_factor(
    lead, high_far, low_far, lower, inverse_high, inverse_low,
    out, matrix, work, down_high, down_low, sems,
):
    copies = (
        pltpu.make_async_copy(high_far, down_high, sems.at[0]),
        pltpu.make_async_copy(low_far, down_low, sems.at[1]),
    )
    for copy in copies:
        copy.start()
    for n, (b, c) in enumerate(UPPER):
        for r in range(16):
            matrix[b * T + 8 * r:b * T + 8 * r + 8, c * T:c * T + T] = lead[r, n]
    out[...] = jnp.zeros_like(out)
    sub = lax.broadcasted_iota(jnp.int32, (8, T), 0)
    eye = (
        lax.broadcasted_iota(jnp.int32, (T, T), 0) == lax.broadcasted_iota(jnp.int32, (T, T), 1)
    ).astype(F32)
    for b in range(PT):
        lo, hi = b * T, b * T + T
        work[:, :T] = matrix[lo:hi, lo:hi]
        work[:, T:] = eye
        for base in range(0, T, GROUP):
            rows = [work[base + 8 * q:base + 8 * q + 8, :T] for q in range(GROUP // 8)]
            other = [work[base + 8 * q:base + 8 * q + 8, T:] for q in range(GROUP // 8)]
            inverses = []
            for p in range(GROUP // 8):
                first = base + 8 * p
                after = range(p, GROUP // 8)
                columns = {
                    q: [
                        jnp.broadcast_to(rows[q][:, first + m:first + m + 1], (8, T))
                        for m in range(8)
                    ]
                    for q in after
                }
                pivots = jnp.ones((8, T), F32)
                for m in range(0, 8, 2):
                    heads = [
                        [jnp.broadcast_to(columns[p][n][r:r + 1, :], (8, T)) for r in (m, m + 1)]
                        for n in range(8)
                    ]
                    (one, side), (_, two) = heads[m], heads[m + 1]
                    over = reciprocal(one * two - side * side)
                    step = side * reciprocal(one)
                    pivots = jnp.where(sub == m, one, pivots)
                    pivots = jnp.where(sub == m + 1, two - side * step, pivots)
                    row, mate = [
                        [jnp.broadcast_to(x[p][r:r + 1, :], (8, T)) for r in (m, m + 1)]
                        for x in (rows, other)
                    ]
                    for q in after:
                        left, right = columns[q][m], columns[q][m + 1]
                        low = (left * two - right * side) * over
                        high = (right * one - left * side) * over
                        if q == p:
                            low = jnp.where(
                                sub > m + 1, low, jnp.where(sub == m + 1, step, 0.0)
                            )
                            high = jnp.where(sub > m + 1, high, 0.0)
                        for n in range(m + 2, 8):
                            columns[q][n] = columns[q][n] - (
                                low * heads[n][0] + high * heads[n][1]
                            )
                        rows[q] = rows[q] - (low * row[0] + high * row[1])
                        other[q] = other[q] - (low * mate[0] + high * mate[1])
                out[lo + first:lo + first + 8, lo:hi] = other[p] * lax.rsqrt(pivots)
                inverses.append(1.0 / pivots)
            if base + GROUP < T:
                scaled = jnp.concatenate([x * y for x, y in zip(rows, inverses)], axis=0)
                both = jnp.concatenate(
                    [jnp.concatenate(rows, axis=0), jnp.concatenate(other, axis=0)], axis=1
                )
                change = jnp.dot(
                    scaled.T[base + GROUP:, :], both,
                    precision=HIGHEST, preferred_element_type=F32,
                )
                work[base + GROUP:, :] = work[base + GROUP:, :] - change
        inverse = out[lo:hi, lo:hi]
        if b > 0:
            out[lo:hi, :lo] = jnp.dot(
                inverse, out[lo:hi, :lo], precision=HIGHEST, preferred_element_type=F32
            )
        if b < PT - 1:
            right = jnp.dot(
                inverse, matrix[lo:hi, hi:], precision=HIGHEST, preferred_element_type=F32
            )
            for n in range(b + 1, PT):
                low, high = n * T, n * T + T
                factor = right[:, low - hi:high - hi]
                matrix[low:high, low:] = matrix[low:high, low:] - lax.dot_general(
                    factor, right[:, low - hi:], (((0,), (0,)), ((), ())),
                    precision=HIGHEST, preferred_element_type=F32,
                )
                out[low:high, :hi] = out[low:high, :hi] - lax.dot_general(
                    factor, out[lo:hi, :hi], (((0,), (0,)), ((), ())),
                    precision=HIGHEST, preferred_element_type=F32,
                )


    high, low = halves(out[...])
    inverse_high[...] = high
    inverse_low[...] = low
    for copy in copies:
        copy.wait()
    for lo, hi in SPLITS:
        lower[:, lo:hi] = product(
            (down_high[:, :hi], down_low[:, :hi]),
            (inverse_high[lo:hi, :hi], inverse_low[lo:hi, :hi]),
            1,
        )


def eliminate(
    maps, front, across_far, lower, inverse_high, inverse_low,
    moved_far, near, rest, out,
    pivot_high, pivot_low, upper, across, moved, other, across_sem, sems,
):
    k, i, j = place()
    row = k * 8 + i
    t = pl.program_id(0)

    def child_copies():
        return (
            pltpu.make_async_copy(moved_far, moved, sems.at[0]),
            pltpu.make_async_copy(near.at[pl.ds(0, 4)], other.at[:, 0], sems.at[1]),
            pltpu.make_async_copy(
                near.at[pl.ds(4, CHILD_TILES - 1)], other.at[0, pl.ds(1, CHILD_TILES - 1)], sems.at[2]
            ),
            pltpu.make_async_copy(
                rest, other.at[pl.ds(1, 3), pl.ds(1, CHILD_TILES - 1)], sems.at[3]
            ),
        )

    @pl.when(t == 0)
    def _():
        arrivals = [
            pltpu.make_async_copy(across_far.at[:, b], across.at[:, b], across_sem.at[b])
            for b in range(PT)
        ]
        for copy in (*arrivals, *child_copies()):
            copy.start()
        for b in range(PT):
            arrivals[b].wait()
            for s in range(COL_TILES):
                tile = across[:, b, s].reshape(T, T)
                high, low = halves(tile)
                pivot_high[b * T:b * T + T, s * T:s * T + T] = high
                pivot_low[b * T:b * T + T, s * T:s * T + T] = low

        for n in range(COL_TILES * T // WIDE):
            part = slice(n * WIDE, n * WIDE + WIDE)
            for lo, hi in SPLITS:
                first, second = inverse_high[lo:hi, :hi], inverse_low[lo:hi, :hi]
                high, low = halves(jnp.dot(
                    jnp.concatenate([first, first, second], axis=1),
                    jnp.concatenate(
                        [pivot_high[:hi, part], pivot_low[:hi, part], pivot_high[:hi, part]], axis=0
                    ),
                    preferred_element_type=F32,
                ))
                upper[lo:hi, part] = high
                upper[PT * T + lo:PT * T + hi, part] = low
                upper[2 * PT * T + lo:2 * PT * T + hi, part] = high

    first, second = halves(lower[...])
    mine = jnp.concatenate([first, first, second], axis=1)
    for n in range(COL_TILES * T // WIDE):
        change = jnp.dot(
            mine, upper[:, n * WIDE:n * WIDE + WIDE], preferred_element_type=F32
        )
        for r in range(BLOCK):
            for s in range(WIDE // T):
                where = pl.ds(r * T * COL_TILES + n * (WIDE // T) + s, T, stride=COL_TILES)
                out[where, :] = front[where, :] - change[r * T:r * T + T, s * T:s * T + T]

    @pl.when(t == 0)
    def _():
        for copy in child_copies():
            copy.wait()

    add_children(maps, moved, other, out)

    @pl.when(jnp.logical_and(t == 0, row < PT))
    def _():
        for s in range(COL_TILES):
            out[pl.ds(s, T, stride=COL_TILES), :] = jnp.zeros((T, T), F32)

    @pl.when(j < PT)
    def _():
        for r in range(BLOCK):
            tile = lower[r * T:r * T + T, pl.ds(pl.multiple_of(j * T, T), T)]
            x = lax.broadcasted_iota(jnp.int32, (T, T), 0) + (16 * (BLOCK * t + r) + row) * T
            y = lax.broadcasted_iota(jnp.int32, (T, T), 1) + j * T
            out[pl.ds(r * T * COL_TILES, T, stride=COL_TILES), :] = jnp.where(x >= y, tile, 0.0)


def pack_other(maps, moved, child, front, near, rest, lead):
    k, i, j = place()
    tile = child[pl.ds(0, T, stride=CHILD_TILES), :]
    tile = tile + jnp.where(k == 0, front[pl.ds(0, T, stride=COL_TILES), :], 0.0)
    for v in range(16):
        lead[v] = tile[8 * v:8 * v + 8]
    rank = jnp.int32(0)
    for g in range(CHILD_TILES):
        shift = offset(maps, k, g)
        source = (i - shift) % 8
        leaves = (8 * g + source + shift) // 8 % 2 != k
        here = jnp.minimum(rank, 3)

        @pl.when(leaves)
        def _():
            near[here] = moved[source * 8 + j]

        @pl.when(jnp.logical_and(leaves, rank == 0))
        def _():
            for h in range(1, CHILD_TILES):
                near[3 + h] = moved[source * 8 + (j - offset(maps, k, h)) % 8]

        @pl.when(jnp.logical_and(leaves, rank > 0))
        def _():
            for h in range(1, CHILD_TILES):
                rest[jnp.maximum(here - 1, 0), h - 1] = moved[
                    source * 8 + (j - offset(maps, k, h)) % 8
                ]

        rank = rank + leaves.astype(jnp.int32)


def add_children(maps, moved, other, out):
    k, i, j = place()
    t = pl.program_id(0)

    def add(child, p, tile_of):
        for h in range(CHILD_TILES):
            across = offset(maps, child, h)
            from_j = (j - across) % 8
            first = p // 16 % BLOCK * (T * COL_TILES) + (8 * h + from_j + across) // 8
            where = pl.ds(first, T, stride=COL_TILES)
            out[where, :] = out[where, :] + tile_of(h, from_j)

    rank = jnp.int32(0)
    for g in range(CHILD_TILES):
        shift = offset(maps, k, g)
        source = (i - shift) % 8
        p = 8 * g + source + shift
        mine = p // 8 % 2 == k

        @pl.when(jnp.logical_and(mine, p // 16 // BLOCK == t))
        def _():
            add(k, p, lambda h, from_j: moved[source * 8 + from_j])

        far = 1 - k
        far_shift = offset(maps, far, g)
        far_p = 8 * g + (i - far_shift) % 8 + far_shift
        comes = far_p // 8 % 2 == k
        here = jnp.minimum(rank, 3)

        @pl.when(jnp.logical_and(comes, far_p // 16 // BLOCK == t))
        def _():
            add(far, far_p, lambda h, from_j: other[here, h])

        rank = rank + comes.astype(jnp.int32)


def shards(front, child_updates, child_maps, child_orders):
    front = front.reshape(ROW_TILES * T * COL_TILES, T)
    child = child_updates.reshape(CHILD_TILES * T * CHILD_TILES, T)
    maps = child_maps
    main = pl.pallas_call(
        pack_main,
        out_shape=shape(64, T, T),
        in_specs=[SMEM, SMEM, VMEM],
        out_specs=VMEM,
        compiler_params=params(16),
        name="pack_main",
    )(maps, child_orders, child)
    main = lax.all_to_all(main, ("i", "col"), 0, 0, tiled=True)
    swap = [(0, 1), (1, 0)]
    near, rest, lead = pl.pallas_call(
        pack_other,
        out_shape=(
            shape(3 + CHILD_TILES, T, T), shape(3, CHILD_TILES - 1, T, T), shape(16, 8, T)
        ),
        in_specs=[SMEM, VMEM, VMEM, VMEM],
        out_specs=[VMEM] * 3,
        compiler_params=params(16),
        name="pack_other",
    )(maps, main, child, front)
    lead = lax.all_to_all(lead, ROWS, 0, 0, tiled=True)
    near = lax.ppermute(near, "k", swap)
    rest = lax.ppermute(rest, "k", swap)
    column = pl.pallas_call(
        add_column,
        out_shape=shape(ROW_TILES * T + 8 * PT, T),
        in_specs=[SMEM, VMEM, VMEM, VMEM, VMEM],
        out_specs=VMEM,
        compiler_params=params(16),
        name="add_column",
    )(maps, front, main, near, lead)
    down = lax.all_gather(column, "col")
    rows = pl.pallas_call(
        pack_rows,
        out_shape=shape(16, COL_TILES, 8, T),
        in_specs=[SMEM, ANY, ANY, VMEM],
        out_specs=VMEM,
        scratch_shapes=[
            pltpu.VMEM((COL_TILES, T, T), F32),
            pltpu.VMEM((T * COL_TILES, T), F32),
            pltpu.VMEM((8, T, T), F32),
            pltpu.SemaphoreType.DMA((2,)),
        ],
        compiler_params=params(58),
        name="pack_rows",
    )(maps, front, main, near)
    rows = lax.all_to_all(rows, ROWS, 0, 0, tiled=True)
    slab = pl.pallas_call(
        take_slab,
        out_shape=shape(PT, COL_TILES, 8, T),
        in_specs=[VMEM, ANY],
        out_specs=VMEM,
        compiler_params=params(16),
        name="take_slab",
    )(rows, rest)
    across = lax.all_gather(slab, ROWS)
    lead = pl.pallas_call(
        pack_lead,
        out_shape=shape(16, len(UPPER), 8, T),
        in_specs=[ANY],
        out_specs=VMEM,
        scratch_shapes=[pltpu.VMEM((PT, 8 * PT, T), F32), pltpu.SemaphoreType.DMA],
        compiler_params=params(58),
        name="pack_lead",
    )(down)
    lead = lax.all_to_all(lead, ROWS, 0, 0, tiled=True)
    tall = jax.ShapeDtypeStruct((ROW_TILES * T, PT * T), BF16)
    halved = pl.pallas_call(
        split_rows,
        out_shape=(tall, tall),
        in_specs=[ANY],
        out_specs=[VMEM] * 2,
        scratch_shapes=[
            pltpu.VMEM((PT, ROW_TILES * T, T), F32), pltpu.SemaphoreType.DMA((PT,)),
        ],
        compiler_params=params(40),
        name="split_rows",
    )(down)
    square = jax.ShapeDtypeStruct((PT * T, PT * T), BF16)
    lower, inverse_high, inverse_low = pl.pallas_call(
        invert_factor,
        out_shape=(shape(ROW_TILES * T, PT * T), square, square),
        in_specs=[VMEM, ANY, ANY],
        out_specs=[VMEM] * 3,
        scratch_shapes=[
            pltpu.VMEM((PT * T, PT * T), F32),
            pltpu.VMEM((PT * T, PT * T), F32),
            pltpu.VMEM((T, 2 * T), F32),
            pltpu.VMEM((ROW_TILES * T, PT * T), BF16),
            pltpu.VMEM((ROW_TILES * T, PT * T), BF16),
            pltpu.SemaphoreType.DMA((2,)),
        ],
        compiler_params=params(58),
        cost_estimate=pl.CostEstimate(flops=30 * 10**9, bytes_accessed=8 * 2**20, transcendentals=0),
        name="invert_factor",
    )(lead, *halved)
    block = pl.BlockSpec((BLOCK * T * COL_TILES, T), lambda t: (t, 0))
    out = pl.pallas_call(
        eliminate,
        out_shape=shape(ROW_TILES * T * COL_TILES, T),
        grid=(ROW_TILES // BLOCK,),
        in_specs=[SMEM, block, ANY, pl.BlockSpec((BLOCK * T, PT * T), lambda t: (t, 0))] + [VMEM] * 2 + [ANY] * 3,
        out_specs=block,
        scratch_shapes=[
            pltpu.VMEM((PT * T, COL_TILES * T), BF16),
            pltpu.VMEM((PT * T, COL_TILES * T), BF16),
            pltpu.VMEM((3 * PT * T, COL_TILES * T), BF16),
            pltpu.VMEM((16, PT, COL_TILES, 8, T), F32),
            pltpu.VMEM((64, T, T), F32),
            pltpu.VMEM((4, CHILD_TILES, T, T), F32),
            pltpu.SemaphoreType.DMA((PT,)),
            pltpu.SemaphoreType.DMA((4,)),
        ],
        compiler_params=params(58),
        cost_estimate=pl.CostEstimate(flops=12 * 10**9, bytes_accessed=20 * 2**20, transcendentals=0),
        name="eliminate",
    )(maps, front, across, lower, inverse_high, inverse_low, main, near, rest)
    return out.reshape(ROW_TILES, 1, T, COL_TILES, 1, T)


def solution(mesh):
    split = Mesh(mesh.devices.reshape(2, 8, 8), ("k", "i", "col"))
    tiles = P(None, ROWS, None, None, "col", None)
    return jax.shard_map(
        shards, mesh=split, in_specs=(tiles, tiles, P(), P()), out_specs=tiles, check_vma=False
    )
```

```python
import jax
import jax.numpy as jnp
from jax import lax
from jax.experimental import pallas as pl
from jax.experimental.pallas import tpu as pltpu
from jax.sharding import Mesh
from jax.sharding import PartitionSpec as P

T = 128
PT = 5
ROW_TILES = 6
COL_TILES = 12
CHILD_TILES = 6
ROWS = ("k", "i")
UPPER = [(b, c) for b in range(PT) for c in range(b, PT)]
GROUP = 32
BLOCK = 2
HIGHEST = lax.Precision.HIGHEST
F32 = jnp.float32
BF16 = jnp.bfloat16

VMEM = pl.BlockSpec(memory_space=pltpu.VMEM)
ANY = pl.BlockSpec(memory_space=pl.ANY)
SMEM = pl.BlockSpec(memory_space=pltpu.SMEM)


def shape(*dims):
    return jax.ShapeDtypeStruct(dims, F32)


def params(mib):
    return pltpu.CompilerParams(vmem_limit_bytes=mib * 2**20)


def place():
    return lax.axis_index("k"), lax.axis_index("i"), lax.axis_index("col")


def offset(maps, child, run):
    return maps[child, 8 * run] - 8 * run


def child_tile(child, order, i, j, g, h):
    tile = child[pl.ds(g * T * CHILD_TILES + h, T, stride=CHILD_TILES), :]
    if g == CHILD_TILES - 1:
        rows = lax.broadcasted_iota(jnp.int32, (T, T), 0) + (8 * g + i) * T
        tile = jnp.where(rows < order, tile, 0.0)
    if h == CHILD_TILES - 1:
        cols = lax.broadcasted_iota(jnp.int32, (T, T), 1) + (8 * h + j) * T
        tile = jnp.where(cols < order, tile, 0.0)
    return tile


def pack_main(maps, orders, far, out, child, tiles, came, went):
    k, i, j = place()
    order = orders[k]
    size = T * CHILD_TILES
    arrivals = [
        pltpu.make_async_copy(
            far.at[pl.ds(g * size, size)], child.at[pl.ds(g * size, size)], came.at[g]
        )
        for g in range(CHILD_TILES)
    ]
    for copy in arrivals:
        copy.start()
    sent = []
    for g in range(CHILD_TILES):
        arrivals[g].wait()
        to_i = (i + offset(maps, k, g)) % 8
        for h in range(CHILD_TILES):
            n = g * CHILD_TILES + h
            to_j = (j + offset(maps, k, h)) % 8
            tiles[n] = child_tile(child, order, i, j, g, h)
            copy = pltpu.make_async_copy(tiles.at[n], out.at[to_i * 8 + to_j], went.at[n])
            copy.start()
            sent.append(copy)
    for copy in sent:
        copy.wait()


def add_column(maps, front, moved, other, lead, out):
    k, i, j = place()

    def tile(t):
        return pl.ds(pl.multiple_of(t * T, T), T)

    for b in range(PT):
        first = ROW_TILES * T + 8 * b
        out[first:first + 8, :] = lead[b] + lead[8 + b]
    for t in range(ROW_TILES):
        out[t * T:t * T + T, :] = front[pl.ds(t * T * COL_TILES, T, stride=COL_TILES), :]
    rank = jnp.int32(0)
    for g in range(CHILD_TILES):
        shift = offset(maps, k, g)
        source = (i - shift) % 8
        p = 8 * g + source + shift

        @pl.when(p // 8 % 2 == k)
        def _():
            out[tile(p // 16), :] = out[tile(p // 16), :] + moved[source * 8 + j]

        far_shift = offset(maps, 1 - k, g)
        far_p = 8 * g + (i - far_shift) % 8 + far_shift
        comes = far_p // 8 % 2 == k
        here = jnp.minimum(rank, 3)

        @pl.when(comes)
        def _():
            out[tile(far_p // 16), :] = out[tile(far_p // 16), :] + other[here]

        rank = rank + comes.astype(jnp.int32)


def pack_rows(maps, front_far, moved_far, other, out, tiles, front, moved, sems):
    k, i, j = place()

    @pl.when(jnp.logical_and(k == 0, i < PT))
    def _():
        copies = (
            pltpu.make_async_copy(front_far.at[pl.ds(0, T * COL_TILES)], front, sems.at[0]),
            pltpu.make_async_copy(moved_far.at[pl.ds(i * 8, 8)], moved, sems.at[1]),
        )
        for copy in copies:
            copy.start()
        for copy in copies:
            copy.wait()
        for s in range(COL_TILES):
            tiles[s] = front[pl.ds(s, T, stride=COL_TILES), :]
        for child in range(2):
            for h in range(CHILD_TILES):
                shift = offset(maps, child, h)
                from_j = (j - shift) % 8
                s = (8 * h + from_j + shift) // 8
                if child == 0:
                    tile = moved[from_j]
                else:
                    tile = other[0 if h == 0 else 3 + h]
                tiles[s] = tiles[s] + tile
        for v in range(16):
            for s in range(COL_TILES):
                out[v, s] = tiles[s, 8 * v:8 * v + 8]


def take_slab(rows, other, out):
    for b in range(PT):
        out[b] = rows[b]


def pack_lead(far, out, got, sem):
    copy = pltpu.make_async_copy(
        far.at[pl.ds(0, PT), pl.ds(ROW_TILES * T, 8 * PT)], got, sem
    )
    copy.start()
    copy.wait()
    for n, (b, c) in enumerate(UPPER):
        piece = got[c, 8 * b:8 * b + 8]
        for v in range(16):
            out[v, n] = piece


SPLITS = ((0, 256), (256, 512), (512, 640))
WIDE = 512


def halves(x):
    high = x.astype(BF16)
    return high, (x - high.astype(F32)).astype(BF16)


def product(a, b, over=0):
    (a_high, a_low), (b_high, b_low) = a, b

    def dot(x, y):
        return lax.dot_general(x, y, (((1,), (over,)), ((), ())), preferred_element_type=F32)

    return dot(a_high, b_high) + (dot(a_high, b_low) + dot(a_low, b_high))


def reciprocal(x):
    y = pl.reciprocal(x, approx=True)
    y = y * (2.0 - x * y)
    return y * (2.0 - x * y)


def split_rows(far, down_high, down_low, down, sems):
    copies = [
        pltpu.make_async_copy(far.at[b, pl.ds(0, ROW_TILES * T)], down.at[b], sems.at[b])
        for b in range(PT)
    ]
    for copy in copies:
        copy.start()
    for b in range(PT):
        copies[b].wait()
        high, low = halves(down[b])
        down_high[:, b * T:b * T + T] = high
        down_low[:, b * T:b * T + T] = low


def invert_factor(
    lead, high_far, low_far, lower, inverse_high, inverse_low,
    out, matrix, work, down_high, down_low, sems,
):
    copies = (
        pltpu.make_async_copy(high_far, down_high, sems.at[0]),
        pltpu.make_async_copy(low_far, down_low, sems.at[1]),
    )
    for copy in copies:
        copy.start()
    for n, (b, c) in enumerate(UPPER):
        for r in range(16):
            matrix[b * T + 8 * r:b * T + 8 * r + 8, c * T:c * T + T] = lead[r, n]
    out[...] = jnp.zeros_like(out)
    sub = lax.broadcasted_iota(jnp.int32, (8, T), 0)
    eye = (
        lax.broadcasted_iota(jnp.int32, (T, T), 0) == lax.broadcasted_iota(jnp.int32, (T, T), 1)
    ).astype(F32)
    for b in range(PT):
        lo, hi = b * T, b * T + T
        work[:, :T] = matrix[lo:hi, lo:hi]
        work[:, T:] = eye
        for base in range(0, T, GROUP):
            rows = [work[base + 8 * q:base + 8 * q + 8, :T] for q in range(GROUP // 8)]
            other = [work[base + 8 * q:base + 8 * q + 8, T:] for q in range(GROUP // 8)]
            inverses = []
            for p in range(GROUP // 8):
                first = base + 8 * p
                after = range(p, GROUP // 8)
                columns = {
                    q: [
                        jnp.broadcast_to(rows[q][:, first + m:first + m + 1], (8, T))
                        for m in range(8)
                    ]
                    for q in after
                }
                pivots = jnp.ones((8, T), F32)
                for m in range(0, 8, 2):
                    heads = [
                        [jnp.broadcast_to(columns[p][n][r:r + 1, :], (8, T)) for r in (m, m + 1)]
                        for n in range(8)
                    ]
                    (one, side), (_, two) = heads[m], heads[m + 1]
                    over = reciprocal(one * two - side * side)
                    step = side * reciprocal(one)
                    pivots = jnp.where(sub == m, one, pivots)
                    pivots = jnp.where(sub == m + 1, two - side * step, pivots)
                    row, mate = [
                        [jnp.broadcast_to(x[p][r:r + 1, :], (8, T)) for r in (m, m + 1)]
                        for x in (rows, other)
                    ]
                    for q in after:
                        left, right = columns[q][m], columns[q][m + 1]
                        low = (left * two - right * side) * over
                        high = (right * one - left * side) * over
                        if q == p:
                            low = jnp.where(
                                sub > m + 1, low, jnp.where(sub == m + 1, step, 0.0)
                            )
                            high = jnp.where(sub > m + 1, high, 0.0)
                        for n in range(m + 2, 8):
                            columns[q][n] = columns[q][n] - (
                                low * heads[n][0] + high * heads[n][1]
                            )
                        rows[q] = rows[q] - (low * row[0] + high * row[1])
                        other[q] = other[q] - (low * mate[0] + high * mate[1])
                out[lo + first:lo + first + 8, lo:hi] = other[p] * lax.rsqrt(pivots)
                inverses.append(1.0 / pivots)
            if base + GROUP < T:
                scaled = jnp.concatenate([x * y for x, y in zip(rows, inverses)], axis=0)
                both = jnp.concatenate(
                    [jnp.concatenate(rows, axis=0), jnp.concatenate(other, axis=0)], axis=1
                )
                change = jnp.dot(
                    scaled.T[base + GROUP:, :], both,
                    precision=HIGHEST, preferred_element_type=F32,
                )
                work[base + GROUP:, :] = work[base + GROUP:, :] - change
        inverse = out[lo:hi, lo:hi]
        if b > 0:
            out[lo:hi, :lo] = jnp.dot(
                inverse, out[lo:hi, :lo], precision=HIGHEST, preferred_element_type=F32
            )
        if b < PT - 1:
            right = jnp.dot(
                inverse, matrix[lo:hi, hi:], precision=HIGHEST, preferred_element_type=F32
            )
            for n in range(b + 1, PT):
                low, high = n * T, n * T + T
                factor = right[:, low - hi:high - hi]
                matrix[low:high, low:] = matrix[low:high, low:] - lax.dot_general(
                    factor, right[:, low - hi:], (((0,), (0,)), ((), ())),
                    precision=HIGHEST, preferred_element_type=F32,
                )
                out[low:high, :hi] = out[low:high, :hi] - lax.dot_general(
                    factor, out[lo:hi, :hi], (((0,), (0,)), ((), ())),
                    precision=HIGHEST, preferred_element_type=F32,
                )


    high, low = halves(out[...])
    inverse_high[...] = high
    inverse_low[...] = low
    for copy in copies:
        copy.wait()
    for lo, hi in SPLITS:
        lower[:, lo:hi] = product(
            (down_high[:, :hi], down_low[:, :hi]),
            (inverse_high[lo:hi, :hi], inverse_low[lo:hi, :hi]),
            1,
        )


def eliminate(
    maps, front, across_far, lower, inverse_high, inverse_low,
    moved_far, near, rest, out,
    pivot_high, pivot_low, upper, across, moved, other, across_sem, sems,
):
    k, i, j = place()
    row = k * 8 + i
    t = pl.program_id(0)

    def child_copies():
        return (
            pltpu.make_async_copy(moved_far, moved, sems.at[0]),
            pltpu.make_async_copy(near.at[pl.ds(0, 4)], other.at[:, 0], sems.at[1]),
            pltpu.make_async_copy(
                near.at[pl.ds(4, CHILD_TILES - 1)], other.at[0, pl.ds(1, CHILD_TILES - 1)], sems.at[2]
            ),
            pltpu.make_async_copy(
                rest, other.at[pl.ds(1, 3), pl.ds(1, CHILD_TILES - 1)], sems.at[3]
            ),
        )

    @pl.when(t == 0)
    def _():
        arrivals = [
            pltpu.make_async_copy(across_far.at[:, b], across.at[:, b], across_sem.at[b])
            for b in range(PT)
        ]
        for copy in (*arrivals, *child_copies()):
            copy.start()
        for b in range(PT):
            arrivals[b].wait()
            for s in range(COL_TILES):
                tile = across[:, b, s].reshape(T, T)
                high, low = halves(tile)
                pivot_high[b * T:b * T + T, s * T:s * T + T] = high
                pivot_low[b * T:b * T + T, s * T:s * T + T] = low

        for n in range(COL_TILES * T // WIDE):
            part = slice(n * WIDE, n * WIDE + WIDE)
            for lo, hi in SPLITS:
                first, second = inverse_high[lo:hi, :hi], inverse_low[lo:hi, :hi]
                high, low = halves(jnp.dot(
                    jnp.concatenate([first, first, second], axis=1),
                    jnp.concatenate(
                        [pivot_high[:hi, part], pivot_low[:hi, part], pivot_high[:hi, part]], axis=0
                    ),
                    preferred_element_type=F32,
                ))
                upper[lo:hi, part] = high
                upper[PT * T + lo:PT * T + hi, part] = low
                upper[2 * PT * T + lo:2 * PT * T + hi, part] = high

    first, second = halves(lower[...])
    mine = jnp.concatenate([first, first, second], axis=1)
    for n in range(COL_TILES * T // WIDE):
        change = jnp.dot(
            mine, upper[:, n * WIDE:n * WIDE + WIDE], preferred_element_type=F32
        )
        for r in range(BLOCK):
            for s in range(WIDE // T):
                where = pl.ds(r * T * COL_TILES + n * (WIDE // T) + s, T, stride=COL_TILES)
                out[where, :] = front[where, :] - change[r * T:r * T + T, s * T:s * T + T]

    @pl.when(t == 0)
    def _():
        for copy in child_copies():
            copy.wait()

    add_children(maps, moved, other, out)

    @pl.when(jnp.logical_and(t == 0, row < PT))
    def _():
        for s in range(COL_TILES):
            out[pl.ds(s, T, stride=COL_TILES), :] = jnp.zeros((T, T), F32)

    @pl.when(j < PT)
    def _():
        for r in range(BLOCK):
            tile = lower[r * T:r * T + T, pl.ds(pl.multiple_of(j * T, T), T)]
            x = lax.broadcasted_iota(jnp.int32, (T, T), 0) + (16 * (BLOCK * t + r) + row) * T
            y = lax.broadcasted_iota(jnp.int32, (T, T), 1) + j * T
            out[pl.ds(r * T * COL_TILES, T, stride=COL_TILES), :] = jnp.where(x >= y, tile, 0.0)


def pack_other(maps, moved, child, front, near, rest, lead):
    k, i, j = place()
    tile = child[pl.ds(0, T, stride=CHILD_TILES), :]
    tile = tile + jnp.where(k == 0, front[pl.ds(0, T, stride=COL_TILES), :], 0.0)
    for v in range(16):
        lead[v] = tile[8 * v:8 * v + 8]
    rank = jnp.int32(0)
    for g in range(CHILD_TILES):
        shift = offset(maps, k, g)
        source = (i - shift) % 8
        leaves = (8 * g + source + shift) // 8 % 2 != k
        here = jnp.minimum(rank, 3)

        @pl.when(leaves)
        def _():
            near[here] = moved[source * 8 + j]

        @pl.when(jnp.logical_and(leaves, rank == 0))
        def _():
            for h in range(1, CHILD_TILES):
                near[3 + h] = moved[source * 8 + (j - offset(maps, k, h)) % 8]

        @pl.when(jnp.logical_and(leaves, rank > 0))
        def _():
            for h in range(1, CHILD_TILES):
                rest[jnp.maximum(here - 1, 0), h - 1] = moved[
                    source * 8 + (j - offset(maps, k, h)) % 8
                ]

        rank = rank + leaves.astype(jnp.int32)


def add_children(maps, moved, other, out):
    k, i, j = place()
    t = pl.program_id(0)

    def add(child, p, tile_of):
        for h in range(CHILD_TILES):
            across = offset(maps, child, h)
            from_j = (j - across) % 8
            first = p // 16 % BLOCK * (T * COL_TILES) + (8 * h + from_j + across) // 8
            where = pl.ds(first, T, stride=COL_TILES)
            out[where, :] = out[where, :] + tile_of(h, from_j)

    rank = jnp.int32(0)
    for g in range(CHILD_TILES):
        shift = offset(maps, k, g)
        source = (i - shift) % 8
        p = 8 * g + source + shift
        mine = p // 8 % 2 == k

        @pl.when(jnp.logical_and(mine, p // 16 // BLOCK == t))
        def _():
            add(k, p, lambda h, from_j: moved[source * 8 + from_j])

        far = 1 - k
        far_shift = offset(maps, far, g)
        far_p = 8 * g + (i - far_shift) % 8 + far_shift
        comes = far_p // 8 % 2 == k
        here = jnp.minimum(rank, 3)

        @pl.when(jnp.logical_and(comes, far_p // 16 // BLOCK == t))
        def _():
            add(far, far_p, lambda h, from_j: other[here, h])

        rank = rank + comes.astype(jnp.int32)


def shards(front, child_updates, child_maps, child_orders):
    front = front.reshape(ROW_TILES * T * COL_TILES, T)
    child = child_updates.reshape(CHILD_TILES * T * CHILD_TILES, T)
    maps = child_maps
    main = pl.pallas_call(
        pack_main,
        out_shape=shape(64, T, T),
        in_specs=[SMEM, SMEM, ANY],
        out_specs=ANY,
        scratch_shapes=[
            pltpu.VMEM((CHILD_TILES * T * CHILD_TILES, T), F32),
            pltpu.VMEM((CHILD_TILES * CHILD_TILES, T, T), F32),
            pltpu.SemaphoreType.DMA((CHILD_TILES,)),
            pltpu.SemaphoreType.DMA((CHILD_TILES * CHILD_TILES,)),
        ],
        compiler_params=params(58),
        name="pack_main",
    )(maps, child_orders, child)
    main = lax.all_to_all(main, ("i", "col"), 0, 0, tiled=True)
    swap = [(0, 1), (1, 0)]
    near, rest, lead = pl.pallas_call(
        pack_other,
        out_shape=(
            shape(3 + CHILD_TILES, T, T), shape(3, CHILD_TILES - 1, T, T), shape(16, 8, T)
        ),
        in_specs=[SMEM, VMEM, VMEM, VMEM],
        out_specs=[VMEM] * 3,
        compiler_params=params(16),
        name="pack_other",
    )(maps, main, child, front)
    lead = lax.all_to_all(lead, ROWS, 0, 0, tiled=True)
    near = lax.ppermute(near, "k", swap)
    rest = lax.ppermute(rest, "k", swap)
    column = pl.pallas_call(
        add_column,
        out_shape=shape(ROW_TILES * T + 8 * PT, T),
        in_specs=[SMEM, VMEM, VMEM, VMEM, VMEM],
        out_specs=VMEM,
        compiler_params=params(16),
        name="add_column",
    )(maps, front, main, near, lead)
    down = lax.all_gather(column, "col")
    rows = pl.pallas_call(
        pack_rows,
        out_shape=shape(16, COL_TILES, 8, T),
        in_specs=[SMEM, ANY, ANY, VMEM],
        out_specs=VMEM,
        scratch_shapes=[
            pltpu.VMEM((COL_TILES, T, T), F32),
            pltpu.VMEM((T * COL_TILES, T), F32),
            pltpu.VMEM((8, T, T), F32),
            pltpu.SemaphoreType.DMA((2,)),
        ],
        compiler_params=params(58),
        name="pack_rows",
    )(maps, front, main, near)
    rows = lax.all_to_all(rows, ROWS, 0, 0, tiled=True)
    slab = pl.pallas_call(
        take_slab,
        out_shape=shape(PT, COL_TILES, 8, T),
        in_specs=[VMEM, ANY],
        out_specs=VMEM,
        compiler_params=params(16),
        name="take_slab",
    )(rows, rest)
    across = lax.all_gather(slab, ROWS)
    lead = pl.pallas_call(
        pack_lead,
        out_shape=shape(16, len(UPPER), 8, T),
        in_specs=[ANY],
        out_specs=VMEM,
        scratch_shapes=[pltpu.VMEM((PT, 8 * PT, T), F32), pltpu.SemaphoreType.DMA],
        compiler_params=params(58),
        name="pack_lead",
    )(down)
    lead = lax.all_to_all(lead, ROWS, 0, 0, tiled=True)
    tall = jax.ShapeDtypeStruct((ROW_TILES * T, PT * T), BF16)
    halved = pl.pallas_call(
        split_rows,
        out_shape=(tall, tall),
        in_specs=[ANY],
        out_specs=[VMEM] * 2,
        scratch_shapes=[
            pltpu.VMEM((PT, ROW_TILES * T, T), F32), pltpu.SemaphoreType.DMA((PT,)),
        ],
        compiler_params=params(40),
        name="split_rows",
    )(down)
    square = jax.ShapeDtypeStruct((PT * T, PT * T), BF16)
    lower, inverse_high, inverse_low = pl.pallas_call(
        invert_factor,
        out_shape=(shape(ROW_TILES * T, PT * T), square, square),
        in_specs=[VMEM, ANY, ANY],
        out_specs=[VMEM] * 3,
        scratch_shapes=[
            pltpu.VMEM((PT * T, PT * T), F32),
            pltpu.VMEM((PT * T, PT * T), F32),
            pltpu.VMEM((T, 2 * T), F32),
            pltpu.VMEM((ROW_TILES * T, PT * T), BF16),
            pltpu.VMEM((ROW_TILES * T, PT * T), BF16),
            pltpu.SemaphoreType.DMA((2,)),
        ],
        compiler_params=params(58),
        cost_estimate=pl.CostEstimate(flops=30 * 10**9, bytes_accessed=8 * 2**20, transcendentals=0),
        name="invert_factor",
    )(lead, *halved)
    block = pl.BlockSpec((BLOCK * T * COL_TILES, T), lambda t: (t, 0))
    out = pl.pallas_call(
        eliminate,
        out_shape=shape(ROW_TILES * T * COL_TILES, T),
        grid=(ROW_TILES // BLOCK,),
        in_specs=[SMEM, block, ANY, pl.BlockSpec((BLOCK * T, PT * T), lambda t: (t, 0))] + [VMEM] * 2 + [ANY] * 3,
        out_specs=block,
        scratch_shapes=[
            pltpu.VMEM((PT * T, COL_TILES * T), BF16),
            pltpu.VMEM((PT * T, COL_TILES * T), BF16),
            pltpu.VMEM((3 * PT * T, COL_TILES * T), BF16),
            pltpu.VMEM((16, PT, COL_TILES, 8, T), F32),
            pltpu.VMEM((64, T, T), F32),
            pltpu.VMEM((4, CHILD_TILES, T, T), F32),
            pltpu.SemaphoreType.DMA((PT,)),
            pltpu.SemaphoreType.DMA((4,)),
        ],
        compiler_params=params(58),
        cost_estimate=pl.CostEstimate(flops=12 * 10**9, bytes_accessed=20 * 2**20, transcendentals=0),
        name="eliminate",
    )(maps, front, across, lower, inverse_high, inverse_low, main, near, rest)
    return out.reshape(ROW_TILES, 1, T, COL_TILES, 1, T)


def solution(mesh):
    split = Mesh(mesh.devices.reshape(2, 8, 8), ("k", "i", "col"))
    tiles = P(None, ROWS, None, None, "col", None)
    return jax.shard_map(
        shards, mesh=split, in_specs=(tiles, tiles, P(), P()), out_specs=tiles, check_vma=False
    )
```

```python
import jax
import jax.numpy as jnp
from jax import lax
from jax.experimental import pallas as pl
from jax.experimental.pallas import tpu as pltpu
from jax.sharding import Mesh
from jax.sharding import PartitionSpec as P

T = 128
PT = 5
ROW_TILES = 6
COL_TILES = 12
CHILD_TILES = 6
ROWS = ("k", "i")
UPPER = [(b, c) for b in range(PT) for c in range(b, PT)]
GROUP = 32
BLOCK = 3
HIGHEST = lax.Precision.HIGHEST
F32 = jnp.float32
BF16 = jnp.bfloat16

VMEM = pl.BlockSpec(memory_space=pltpu.VMEM)
ANY = pl.BlockSpec(memory_space=pl.ANY)
SMEM = pl.BlockSpec(memory_space=pltpu.SMEM)


def shape(*dims):
    return jax.ShapeDtypeStruct(dims, F32)


def params(mib):
    return pltpu.CompilerParams(vmem_limit_bytes=mib * 2**20)


def place():
    return lax.axis_index("k"), lax.axis_index("i"), lax.axis_index("col")


def offset(maps, child, run):
    return maps[child, 8 * run] - 8 * run


def child_tile(child, order, i, j, g, h):
    tile = child[pl.ds(g * T * CHILD_TILES + h, T, stride=CHILD_TILES), :]
    if g == CHILD_TILES - 1:
        rows = lax.broadcasted_iota(jnp.int32, (T, T), 0) + (8 * g + i) * T
        tile = jnp.where(rows < order, tile, 0.0)
    if h == CHILD_TILES - 1:
        cols = lax.broadcasted_iota(jnp.int32, (T, T), 1) + (8 * h + j) * T
        tile = jnp.where(cols < order, tile, 0.0)
    return tile


def pack_main(maps, orders, child, out):
    k, i, j = place()
    order = orders[k]
    for g in range(CHILD_TILES):
        to_i = (i + offset(maps, k, g)) % 8
        for h in range(CHILD_TILES):
            to_j = (j + offset(maps, k, h)) % 8
            out[to_i * 8 + to_j] = child_tile(child, order, i, j, g, h)


def add_column(maps, front, moved, other, lead, out):
    k, i, j = place()

    def tile(t):
        return pl.ds(pl.multiple_of(t * T, T), T)

    for b in range(PT):
        first = ROW_TILES * T + 8 * b
        out[first:first + 8, :] = lead[b] + lead[8 + b]
    for t in range(ROW_TILES):
        out[t * T:t * T + T, :] = front[pl.ds(t * T * COL_TILES, T, stride=COL_TILES), :]
    rank = jnp.int32(0)
    for g in range(CHILD_TILES):
        shift = offset(maps, k, g)
        source = (i - shift) % 8
        p = 8 * g + source + shift

        @pl.when(p // 8 % 2 == k)
        def _():
            out[tile(p // 16), :] = out[tile(p // 16), :] + moved[source * 8 + j]

        far_shift = offset(maps, 1 - k, g)
        far_p = 8 * g + (i - far_shift) % 8 + far_shift
        comes = far_p // 8 % 2 == k
        here = jnp.minimum(rank, 3)

        @pl.when(comes)
        def _():
            out[tile(far_p // 16), :] = out[tile(far_p // 16), :] + other[here]

        rank = rank + comes.astype(jnp.int32)


def pack_rows(maps, front_far, moved_far, other, out, tiles, front, moved, sems):
    k, i, j = place()

    @pl.when(jnp.logical_and(k == 0, i < PT))
    def _():
        copies = (
            pltpu.make_async_copy(front_far.at[pl.ds(0, T * COL_TILES)], front, sems.at[0]),
            pltpu.make_async_copy(moved_far.at[pl.ds(i * 8, 8)], moved, sems.at[1]),
        )
        for copy in copies:
            copy.start()
        for copy in copies:
            copy.wait()
        for s in range(COL_TILES):
            tiles[s] = front[pl.ds(s, T, stride=COL_TILES), :]
        for child in range(2):
            for h in range(CHILD_TILES):
                shift = offset(maps, child, h)
                from_j = (j - shift) % 8
                s = (8 * h + from_j + shift) // 8
                if child == 0:
                    tile = moved[from_j]
                else:
                    tile = other[0 if h == 0 else 3 + h]
                tiles[s] = tiles[s] + tile
        for v in range(16):
            for s in range(COL_TILES):
                out[v, s] = tiles[s, 8 * v:8 * v + 8]


def take_slab(rows, other, lead, out):
    for b in range(PT):
        out[b] = rows[b]


def pack_lead(far, out, got, sem):
    copy = pltpu.make_async_copy(
        far.at[pl.ds(0, PT), pl.ds(ROW_TILES * T, 8 * PT)], got, sem
    )
    copy.start()
    copy.wait()
    for n, (b, c) in enumerate(UPPER):
        piece = got[c, 8 * b:8 * b + 8]
        for v in range(16):
            out[v, n] = piece


SPLITS = ((0, 256), (256, 512), (512, 640))
WIDE = 512


def halves(x):
    high = x.astype(BF16)
    return high, (x - high.astype(F32)).astype(BF16)


def product(a, b, over=0):
    (a_high, a_low), (b_high, b_low) = a, b

    def dot(x, y):
        return lax.dot_general(x, y, (((1,), (over,)), ((), ())), preferred_element_type=F32)

    return dot(a_high, b_high) + (dot(a_high, b_low) + dot(a_low, b_high))


def reciprocal(x):
    y = pl.reciprocal(x, approx=True)
    y = y * (2.0 - x * y)
    return y * (2.0 - x * y)


def split_rows(far, down_high, down_low, down, sems):
    copies = [
        pltpu.make_async_copy(far.at[b, pl.ds(0, ROW_TILES * T)], down.at[b], sems.at[b])
        for b in range(PT)
    ]
    for copy in copies:
        copy.start()
    for b in range(PT):
        copies[b].wait()
        high, low = halves(down[b])
        down_high[:, b * T:b * T + T] = high
        down_low[:, b * T:b * T + T] = low


def invert_factor(
    lead, high_far, low_far, lower, inverse_high, inverse_low,
    out, matrix, work, down_high, down_low, sems,
):
    copies = (
        pltpu.make_async_copy(high_far, down_high, sems.at[0]),
        pltpu.make_async_copy(low_far, down_low, sems.at[1]),
    )
    for copy in copies:
        copy.start()
    for n, (b, c) in enumerate(UPPER):
        for r in range(16):
            matrix[b * T + 8 * r:b * T + 8 * r + 8, c * T:c * T + T] = lead[r, n]
    out[...] = jnp.zeros_like(out)
    sub = lax.broadcasted_iota(jnp.int32, (8, T), 0)
    eye = (
        lax.broadcasted_iota(jnp.int32, (T, T), 0) == lax.broadcasted_iota(jnp.int32, (T, T), 1)
    ).astype(F32)
    for b in range(PT):
        lo, hi = b * T, b * T + T
        work[:, :T] = matrix[lo:hi, lo:hi]
        work[:, T:] = eye
        for base in range(0, T, GROUP):
            rows = [work[base + 8 * q:base + 8 * q + 8, :T] for q in range(GROUP // 8)]
            other = [work[base + 8 * q:base + 8 * q + 8, T:] for q in range(GROUP // 8)]
            inverses = []
            for p in range(GROUP // 8):
                first = base + 8 * p
                after = range(p, GROUP // 8)
                columns = {
                    q: [
                        jnp.broadcast_to(rows[q][:, first + m:first + m + 1], (8, T))
                        for m in range(8)
                    ]
                    for q in after
                }
                pivots = jnp.ones((8, T), F32)
                for m in range(0, 8, 2):
                    heads = [
                        [jnp.broadcast_to(columns[p][n][r:r + 1, :], (8, T)) for r in (m, m + 1)]
                        for n in range(8)
                    ]
                    (one, side), (_, two) = heads[m], heads[m + 1]
                    over = reciprocal(one * two - side * side)
                    step = side * reciprocal(one)
                    pivots = jnp.where(sub == m, one, pivots)
                    pivots = jnp.where(sub == m + 1, two - side * step, pivots)
                    row, mate = [
                        [jnp.broadcast_to(x[p][r:r + 1, :], (8, T)) for r in (m, m + 1)]
                        for x in (rows, other)
                    ]
                    for q in after:
                        left, right = columns[q][m], columns[q][m + 1]
                        low = (left * two - right * side) * over
                        high = (right * one - left * side) * over
                        if q == p:
                            low = jnp.where(
                                sub > m + 1, low, jnp.where(sub == m + 1, step, 0.0)
                            )
                            high = jnp.where(sub > m + 1, high, 0.0)
                        for n in range(m + 2, 8):
                            columns[q][n] = columns[q][n] - (
                                low * heads[n][0] + high * heads[n][1]
                            )
                        rows[q] = rows[q] - (low * row[0] + high * row[1])
                        other[q] = other[q] - (low * mate[0] + high * mate[1])
                out[lo + first:lo + first + 8, lo:hi] = other[p] * lax.rsqrt(pivots)
                inverses.append(1.0 / pivots)
            if base + GROUP < T:
                scaled = jnp.concatenate([x * y for x, y in zip(rows, inverses)], axis=0)
                both = jnp.concatenate(
                    [jnp.concatenate(rows, axis=0), jnp.concatenate(other, axis=0)], axis=1
                )
                change = jnp.dot(
                    scaled.T[base + GROUP:, :], both,
                    precision=HIGHEST, preferred_element_type=F32,
                )
                work[base + GROUP:, :] = work[base + GROUP:, :] - change
        inverse = out[lo:hi, lo:hi]
        if b > 0:
            out[lo:hi, :lo] = jnp.dot(
                inverse, out[lo:hi, :lo], precision=HIGHEST, preferred_element_type=F32
            )
        if b < PT - 1:
            right = jnp.dot(
                inverse, matrix[lo:hi, hi:], precision=HIGHEST, preferred_element_type=F32
            )
            for n in range(b + 1, PT):
                low, high = n * T, n * T + T
                factor = right[:, low - hi:high - hi]
                matrix[low:high, low:] = matrix[low:high, low:] - lax.dot_general(
                    factor, right[:, low - hi:], (((0,), (0,)), ((), ())),
                    precision=HIGHEST, preferred_element_type=F32,
                )
                out[low:high, :hi] = out[low:high, :hi] - lax.dot_general(
                    factor, out[lo:hi, :hi], (((0,), (0,)), ((), ())),
                    precision=HIGHEST, preferred_element_type=F32,
                )


    high, low = halves(out[...])
    inverse_high[...] = high
    inverse_low[...] = low
    for copy in copies:
        copy.wait()
    for lo, hi in SPLITS:
        lower[:, lo:hi] = product(
            (down_high[:, :hi], down_low[:, :hi]),
            (inverse_high[lo:hi, :hi], inverse_low[lo:hi, :hi]),
            1,
        )


def eliminate(
    maps, front, across_far, lower, inverse_high, inverse_low,
    moved_far, near, rest, out,
    pivot_high, pivot_low, upper, across, moved, other, across_sem, sems,
):
    k, i, j = place()
    row = k * 8 + i
    t = pl.program_id(0)

    def child_copies():
        return (
            pltpu.make_async_copy(moved_far, moved, sems.at[0]),
            pltpu.make_async_copy(near.at[pl.ds(0, 4)], other.at[:, 0], sems.at[1]),
            pltpu.make_async_copy(
                near.at[pl.ds(4, CHILD_TILES - 1)], other.at[0, pl.ds(1, CHILD_TILES - 1)], sems.at[2]
            ),
            pltpu.make_async_copy(
                rest, other.at[pl.ds(1, 3), pl.ds(1, CHILD_TILES - 1)], sems.at[3]
            ),
        )

    @pl.when(t == 0)
    def _():
        arrivals = [
            pltpu.make_async_copy(across_far.at[:, b], across.at[:, b], across_sem.at[b])
            for b in range(PT)
        ]
        for copy in (*arrivals, *child_copies()):
            copy.start()
        for b in range(PT):
            arrivals[b].wait()
            for s in range(COL_TILES):
                tile = across[:, b, s].reshape(T, T)
                high, low = halves(tile)
                pivot_high[b * T:b * T + T, s * T:s * T + T] = high
                pivot_low[b * T:b * T + T, s * T:s * T + T] = low

        for n in range(COL_TILES * T // WIDE):
            part = slice(n * WIDE, n * WIDE + WIDE)
            for lo, hi in SPLITS:
                first, second = inverse_high[lo:hi, :hi], inverse_low[lo:hi, :hi]
                high, low = halves(jnp.dot(
                    jnp.concatenate([first, first, second], axis=1),
                    jnp.concatenate(
                        [pivot_high[:hi, part], pivot_low[:hi, part], pivot_high[:hi, part]], axis=0
                    ),
                    preferred_element_type=F32,
                ))
                upper[lo:hi, part] = high
                upper[PT * T + lo:PT * T + hi, part] = low
                upper[2 * PT * T + lo:2 * PT * T + hi, part] = high

    first, second = halves(lower[...])
    mine = jnp.concatenate([first, first, second], axis=1)
    for n in range(COL_TILES * T // WIDE):
        change = jnp.dot(
            mine, upper[:, n * WIDE:n * WIDE + WIDE], preferred_element_type=F32
        )
        for r in range(BLOCK):
            for s in range(WIDE // T):
                where = pl.ds(r * T * COL_TILES + n * (WIDE // T) + s, T, stride=COL_TILES)
                out[where, :] = front[where, :] - change[r * T:r * T + T, s * T:s * T + T]

    @pl.when(t == 0)
    def _():
        for copy in child_copies():
            copy.wait()

    add_children(maps, moved, other, out)

    @pl.when(jnp.logical_and(t == 0, row < PT))
    def _():
        for s in range(COL_TILES):
            out[pl.ds(s, T, stride=COL_TILES), :] = jnp.zeros((T, T), F32)

    @pl.when(j < PT)
    def _():
        for r in range(BLOCK):
            tile = lower[r * T:r * T + T, pl.ds(pl.multiple_of(j * T, T), T)]
            x = lax.broadcasted_iota(jnp.int32, (T, T), 0) + (16 * (BLOCK * t + r) + row) * T
            y = lax.broadcasted_iota(jnp.int32, (T, T), 1) + j * T
            out[pl.ds(r * T * COL_TILES, T, stride=COL_TILES), :] = jnp.where(x >= y, tile, 0.0)


def pack_other(maps, moved, child, front, near, rest, lead):
    k, i, j = place()
    tile = child[pl.ds(0, T, stride=CHILD_TILES), :]
    tile = tile + jnp.where(k == 0, front[pl.ds(0, T, stride=COL_TILES), :], 0.0)
    for v in range(16):
        lead[v] = tile[8 * v:8 * v + 8]
    rank = jnp.int32(0)
    for g in range(CHILD_TILES):
        shift = offset(maps, k, g)
        source = (i - shift) % 8
        leaves = (8 * g + source + shift) // 8 % 2 != k
        here = jnp.minimum(rank, 3)

        @pl.when(leaves)
        def _():
            near[here] = moved[source * 8 + j]

        @pl.when(jnp.logical_and(leaves, rank == 0))
        def _():
            for h in range(1, CHILD_TILES):
                near[3 + h] = moved[source * 8 + (j - offset(maps, k, h)) % 8]

        @pl.when(jnp.logical_and(leaves, rank > 0))
        def _():
            for h in range(1, CHILD_TILES):
                rest[jnp.maximum(here - 1, 0), h - 1] = moved[
                    source * 8 + (j - offset(maps, k, h)) % 8
                ]

        rank = rank + leaves.astype(jnp.int32)


def add_children(maps, moved, other, out):
    k, i, j = place()
    t = pl.program_id(0)

    def add(child, p, tile_of):
        for h in range(CHILD_TILES):
            across = offset(maps, child, h)
            from_j = (j - across) % 8
            first = p // 16 % BLOCK * (T * COL_TILES) + (8 * h + from_j + across) // 8
            where = pl.ds(first, T, stride=COL_TILES)
            out[where, :] = out[where, :] + tile_of(h, from_j)

    rank = jnp.int32(0)
    for g in range(CHILD_TILES):
        shift = offset(maps, k, g)
        source = (i - shift) % 8
        p = 8 * g + source + shift
        mine = p // 8 % 2 == k

        @pl.when(jnp.logical_and(mine, p // 16 // BLOCK == t))
        def _():
            add(k, p, lambda h, from_j: moved[source * 8 + from_j])

        far = 1 - k
        far_shift = offset(maps, far, g)
        far_p = 8 * g + (i - far_shift) % 8 + far_shift
        comes = far_p // 8 % 2 == k
        here = jnp.minimum(rank, 3)

        @pl.when(jnp.logical_and(comes, far_p // 16 // BLOCK == t))
        def _():
            add(far, far_p, lambda h, from_j: other[here, h])

        rank = rank + comes.astype(jnp.int32)


def shards(front, child_updates, child_maps, child_orders):
    front = front.reshape(ROW_TILES * T * COL_TILES, T)
    child = child_updates.reshape(CHILD_TILES * T * CHILD_TILES, T)
    maps = child_maps
    main = pl.pallas_call(
        pack_main,
        out_shape=shape(64, T, T),
        in_specs=[SMEM, SMEM, VMEM],
        out_specs=VMEM,
        compiler_params=params(16),
        name="pack_main",
    )(maps, child_orders, child)
    main = lax.all_to_all(main, ("i", "col"), 0, 0, tiled=True)
    swap = [(0, 1), (1, 0)]
    near, rest, lead = pl.pallas_call(
        pack_other,
        out_shape=(
            shape(3 + CHILD_TILES, T, T), shape(3, CHILD_TILES - 1, T, T), shape(16, 8, T)
        ),
        in_specs=[SMEM, VMEM, VMEM, VMEM],
        out_specs=[VMEM] * 3,
        compiler_params=params(16),
        name="pack_other",
    )(maps, main, child, front)
    lead = lax.all_to_all(lead, ROWS, 0, 0, tiled=True)
    near = lax.ppermute(near, "k", swap)
    rest = lax.ppermute(rest, "k", swap)
    column = pl.pallas_call(
        add_column,
        out_shape=shape(ROW_TILES * T + 8 * PT, T),
        in_specs=[SMEM, VMEM, VMEM, VMEM, VMEM],
        out_specs=VMEM,
        compiler_params=params(16),
        name="add_column",
    )(maps, front, main, near, lead)
    down = lax.all_gather(column, "col")
    rows = pl.pallas_call(
        pack_rows,
        out_shape=shape(16, COL_TILES, 8, T),
        in_specs=[SMEM, ANY, ANY, VMEM],
        out_specs=VMEM,
        scratch_shapes=[
            pltpu.VMEM((COL_TILES, T, T), F32),
            pltpu.VMEM((T * COL_TILES, T), F32),
            pltpu.VMEM((8, T, T), F32),
            pltpu.SemaphoreType.DMA((2,)),
        ],
        compiler_params=params(58),
        name="pack_rows",
    )(maps, front, main, near)
    rows = lax.all_to_all(rows, ROWS, 0, 0, tiled=True)
    lead = pl.pallas_call(
        pack_lead,
        out_shape=shape(16, len(UPPER), 8, T),
        in_specs=[ANY],
        out_specs=VMEM,
        scratch_shapes=[pltpu.VMEM((PT, 8 * PT, T), F32), pltpu.SemaphoreType.DMA],
        compiler_params=params(58),
        name="pack_lead",
    )(down)
    slab = pl.pallas_call(
        take_slab,
        out_shape=shape(PT, COL_TILES, 8, T),
        in_specs=[VMEM, ANY, ANY],
        out_specs=VMEM,
        compiler_params=params(16),
        name="take_slab",
    )(rows, rest, lead)
    across = lax.all_gather(slab, ROWS)
    lead = lax.all_to_all(lead, ROWS, 0, 0, tiled=True)
    tall = jax.ShapeDtypeStruct((ROW_TILES * T, PT * T), BF16)
    halved = pl.pallas_call(
        split_rows,
        out_shape=(tall, tall),
        in_specs=[ANY],
        out_specs=[VMEM] * 2,
        scratch_shapes=[
            pltpu.VMEM((PT, ROW_TILES * T, T), F32), pltpu.SemaphoreType.DMA((PT,)),
        ],
        compiler_params=params(40),
        name="split_rows",
    )(down)
    square = jax.ShapeDtypeStruct((PT * T, PT * T), BF16)
    lower, inverse_high, inverse_low = pl.pallas_call(
        invert_factor,
        out_shape=(shape(ROW_TILES * T, PT * T), square, square),
        in_specs=[VMEM, ANY, ANY],
        out_specs=[VMEM] * 3,
        scratch_shapes=[
            pltpu.VMEM((PT * T, PT * T), F32),
            pltpu.VMEM((PT * T, PT * T), F32),
            pltpu.VMEM((T, 2 * T), F32),
            pltpu.VMEM((ROW_TILES * T, PT * T), BF16),
            pltpu.VMEM((ROW_TILES * T, PT * T), BF16),
            pltpu.SemaphoreType.DMA((2,)),
        ],
        compiler_params=params(58),
        cost_estimate=pl.CostEstimate(flops=30 * 10**9, bytes_accessed=8 * 2**20, transcendentals=0),
        name="invert_factor",
    )(lead, *halved)
    block = pl.BlockSpec((BLOCK * T * COL_TILES, T), lambda t: (t, 0))
    out = pl.pallas_call(
        eliminate,
        out_shape=shape(ROW_TILES * T * COL_TILES, T),
        grid=(ROW_TILES // BLOCK,),
        in_specs=[SMEM, block, ANY, pl.BlockSpec((BLOCK * T, PT * T), lambda t: (t, 0))] + [VMEM] * 2 + [ANY] * 3,
        out_specs=block,
        scratch_shapes=[
            pltpu.VMEM((PT * T, COL_TILES * T), BF16),
            pltpu.VMEM((PT * T, COL_TILES * T), BF16),
            pltpu.VMEM((3 * PT * T, COL_TILES * T), BF16),
            pltpu.VMEM((16, PT, COL_TILES, 8, T), F32),
            pltpu.VMEM((64, T, T), F32),
            pltpu.VMEM((4, CHILD_TILES, T, T), F32),
            pltpu.SemaphoreType.DMA((PT,)),
            pltpu.SemaphoreType.DMA((4,)),
        ],
        compiler_params=params(58),
        cost_estimate=pl.CostEstimate(flops=12 * 10**9, bytes_accessed=20 * 2**20, transcendentals=0),
        name="eliminate",
    )(maps, front, across, lower, inverse_high, inverse_low, main, near, rest)
    return out.reshape(ROW_TILES, 1, T, COL_TILES, 1, T)


def solution(mesh):
    split = Mesh(mesh.devices.reshape(2, 8, 8), ("k", "i", "col"))
    tiles = P(None, ROWS, None, None, "col", None)
    return jax.shard_map(
        shards, mesh=split, in_specs=(tiles, tiles, P(), P()), out_specs=tiles, check_vma=False
    )
```
